32 devices in a mesh: gx: 4 (over x, core), gy: 8 (over z, y).
Axes of the slice: x: 2, y: 2, z: 4, core: 2. Of those that a mesh axis runs over, the one named last changes fastest.
Arguments:
- hidden_in: bfloat16 [2048, 4096], P('gx', 'gy')
- norm_gain: bfloat16 [4096], P('gy'), may hold values from 0.099609375 to 1.8984375
- query_proj: bfloat16 [4096, 4096], P('gx', 'gy')
- kv_proj: bfloat16 [1024, 4096], P(None, 'gy')
- prompt_lengths: int32 [8], replicated, may hold values from 1 to 1024, 2048 in all
- cache_slot: int32 [128], replicated, may hold values from 0 to 127, as said below
Outputs:
- attention: bfloat16 [2048, 4096], P('gy', 'gx')
- kv_cache: bfloat16 [128, 16, 1024], P('gy', None, 'gx')
The draws below stay inside these ranges and needn't reach their ends.
Inputs may be any that keep to these rules, and one draw needn't show every extreme that they name: `prompt_lengths`: the 8 prompts sum to 2048 tokens; the longest has exactly 1024. `cache_slot`: A permutation of the 128 slots; slot s is held by index s // 16 of gy. The 16 pages of one token block go to any one index at most 2 times, and every index receives exactly 16 pages.
All inputs are finite; a program needn't handle non-finite values.
Results may differ from the reference program's by a relative error of at most 0.0066.
The reference program's roundings to bfloat16 on the way (of `normed`, `queries` and `rounded`) count: a program that leaves them out, or rounds other values in their place, can miss the bound.
Values may be sent and summed in bfloat16 or wider, within the bound.
A program may use at most 128 MiB of HBM per device.

```python
import math
import jax
import jax.numpy as jnp
import numpy as np
from jax import lax

D = 4096
H = 32
KVH = 4
HD = 128
TOK_BLK = 256
PAGES_DEV = 16
NSEG = 8
TOKENS = 2048
MOST = 1024
PAGE = 16
PAGES = 128


def draw_hidden_in(key, part):
    noise_key = jax.random.fold_in(key, 1)
    row_key = jax.random.fold_in(key, 2)
    column_key = jax.random.fold_in(key, 3)
    column_scale = 3.0 ** (jnp.arange(D, dtype=jnp.float32) / (D - 1)) * jnp.exp(jax.random.uniform(column_key, (D,)) * math.log(10.0))
    noise_draw = jax.random.normal(noise_key, (TOKENS, D))
    row_scale = jnp.exp(jax.random.uniform(row_key, (TOKENS,)) * math.log(10.0))
    return (0.1 * noise_draw * row_scale[:, None] * column_scale[None, :]).astype(jnp.bfloat16)


def kv_matrix(key):
    kv_key = jax.random.fold_in(key, 11)
    noise_draw = jax.random.normal(kv_key, (2 * KVH * HD, D))
    return noise_draw * D ** (-0.5)


def draw_kv_proj(key, part):
    return kv_matrix(key).astype(jnp.bfloat16)


def draw_query_proj(key, part):
    query_key = jax.random.fold_in(key, 12)
    noise_draw = jax.random.normal(query_key, (H * HD, D)) * D ** (-0.5)
    return noise_draw.astype(jnp.bfloat16)


def draw_cache_slot(key, part):
    per_dev = PAGES_DEV
    owner_count = PAGES // PAGES_DEV
    first_perm = jax.random.permutation(jax.random.fold_in(key, 21), owner_count)
    second_perm = jax.random.permutation(jax.random.fold_in(key, 22), owner_count)
    offsets = jax.random.permutation(jax.random.fold_in(key, 23), max(owner_count, per_dev))[:per_dev] % owner_count
    owners = second_perm[(first_perm[:, None] + offsets[None, :]) % owner_count]
    scores = jax.random.randint(jax.random.fold_in(key, 24), (owner_count, per_dev), 0, 1 << 20) * per_dev + jnp.arange(per_dev, dtype=jnp.int32)[None, :]
    order_rank = jnp.argsort(jnp.argsort(scores, axis=1), axis=1)
    local_slot = order_rank[owners, jnp.arange(per_dev, dtype=jnp.int32)[None, :]]
    return (owners * per_dev + local_slot).reshape(-1).astype(jnp.int32)


def length_profile(amount, total, limit, lean):
    weights = [(1 << 20) // math.isqrt(grade ** lean) + 1 for grade in range(2, amount + 1)]
    rest, counts = total - limit - (amount - 1), [1] * (amount - 1)
    while rest > 0:
        candidates = [i for i in range(amount - 1) if counts[i] < limit]
        mass, left = sum([weights[i] for i in candidates]), rest
        for i in candidates:
            extra = min(limit - counts[i], max(1, left * weights[i] // mass), rest)
            counts[i] = counts[i] + extra
            rest = rest - extra
    return np.array([limit] + counts)


def ragged(own_key, count, total, reach, slope):
    if count == 2:
        one = jax.random.randint(own_key, (), max(1, total - reach), min(reach, total - 1) + 1)
        return jnp.stack([one, total - one])
    tallies = jnp.asarray(length_profile(count, total, reach, slope), jnp.int32)
    couples = (count - 1) // 2
    source_of, receiver = tallies[1:1 + 2 * couples:2], tallies[2:2 + 2 * couples:2]
    room = jnp.minimum(source_of - 1, reach - receiver)
    passed = jax.random.randint(jax.random.fold_in(own_key, 1), (couples,), 0, 1 << 20) % (room + 1)
    tallies = tallies.at[1:1 + 2 * couples:2].set(source_of - passed).at[2:2 + 2 * couples:2].set(receiver + passed)
    return tallies[jax.random.permutation(jax.random.fold_in(own_key, 2), count)]


def setup_inputs(seed: int = 0) -> dict:
    arg_keys = jax.random.split(jax.random.key(seed), 7)
    return {
        "hidden_in": draw_hidden_in(jax.random.fold_in(arg_keys[6], 71), 0),
        "norm_gain": jnp.clip(1.0 + 0.18 * jax.random.normal(arg_keys[1], (D,), jnp.float32), 0.099609375, 1.8984375).astype(jnp.bfloat16),
        "query_proj": draw_query_proj(jax.random.fold_in(arg_keys[6], 71), 0),
        "kv_proj": draw_kv_proj(jax.random.fold_in(arg_keys[6], 71), 0),
        "prompt_lengths": ragged(arg_keys[4], NSEG, TOKENS, MOST, 2).astype(jnp.int32),
        "cache_slot": draw_cache_slot(jax.random.fold_in(arg_keys[6], 71), 0),
    }


epsilon = 1e-06
rope_base = 5000000.0
masked_out = -1e+30

def token_places(prompt_lengths, token_index):
    prompt_ends = jnp.cumsum(prompt_lengths).astype(jnp.int32)
    prompt_starts = prompt_ends - prompt_lengths
    segment = lax.optimization_barrier(jnp.sum((token_index[:, None] >= prompt_ends[None, :]).astype(jnp.int32), axis=1))
    chosen = segment[:, None] == jnp.arange(prompt_lengths.shape[0], dtype=jnp.int32)[None, :]
    opening = lax.optimization_barrier(jnp.sum(jnp.where(chosen, prompt_starts[None, :], 0), axis=1)).astype(jnp.int32)
    return (segment, token_index - opening)

def rotate(vectors, places):
    half_size = vectors.shape[-1] // 2
    frequency = rope_base ** (-(jnp.arange(half_size, dtype=jnp.float32) * 2.0) / vectors.shape[-1])
    angles = places.astype(jnp.float32)[:, None] * frequency[None, :]
    cos_part = jnp.cos(angles)[:, None, :]
    sin_part = jnp.sin(angles)[:, None, :]
    leading = vectors[..., :half_size]
    trailing = vectors[..., half_size:]
    return jnp.concatenate([leading * cos_part - trailing * sin_part, trailing * cos_part + leading * sin_part], axis=-1)

def reference(hidden_in, norm_gain, query_proj, kv_proj, prompt_lengths, cache_slot):
    total_tokens = hidden_in.shape[0]
    token_index = jnp.arange(total_tokens, dtype=jnp.int32)
    segment, places = token_places(prompt_lengths, token_index)
    widened = hidden_in.astype(jnp.float32)
    mean_square = lax.optimization_barrier(jnp.mean(widened * widened, axis=1, keepdims=True))
    normed = (widened * lax.rsqrt(mean_square + epsilon) * norm_gain.astype(jnp.float32)[None, :]).astype(jnp.bfloat16)
    contract = (((1,), (1,)), ((), ()))
    query_raw = lax.dot_general(normed, query_proj, contract, preferred_element_type=jnp.float32).reshape(total_tokens, H, HD)
    kv_raw = lax.dot_general(normed, kv_proj, contract, preferred_element_type=jnp.float32).reshape(total_tokens, KVH, 2, HD)
    queries = rotate(query_raw, places).astype(jnp.bfloat16)
    keys = rotate(kv_raw[:, :, 0, :], places).astype(jnp.bfloat16)
    values = kv_raw[:, :, 1, :].astype(jnp.bfloat16)
    group_size = H // KVH
    block_count = total_tokens // TOK_BLK
    score_scale = 1.0 / math.sqrt(HD)

    def one_item(item):
        group_index, block_index = item
        begin = (block_index * TOK_BLK).astype(jnp.int32)
        query_rows = lax.dynamic_slice(queries, (begin, (group_index * group_size).astype(jnp.int32), jnp.int32(0)), (TOK_BLK, group_size, HD))
        key_rows = lax.dynamic_index_in_dim(keys, group_index, 1, keepdims=False)
        value_rows = lax.dynamic_index_in_dim(values, group_index, 1, keepdims=False)
        query_segment = lax.dynamic_slice_in_dim(segment, begin, TOK_BLK, 0)
        query_index = begin + jnp.arange(TOK_BLK, dtype=jnp.int32)
        allowed = (segment[None, :] == query_segment[:, None]) & (token_index[None, :] <= query_index[:, None])
        scores = jnp.einsum('qhd,kd->hqk', query_rows.astype(jnp.float32), key_rows.astype(jnp.float32)) * score_scale
        scores = jnp.where(allowed[None], scores, masked_out)
        row_max = lax.optimization_barrier(jnp.max(scores, axis=2, keepdims=True))
        weights = jnp.where(allowed[None], jnp.exp(scores - row_max), 0.0)
        totals = lax.optimization_barrier(jnp.sum(weights, axis=2))
        rounded = lax.optimization_barrier(weights.astype(jnp.bfloat16)).astype(jnp.float32)
        mixed = jnp.einsum('hqk,kd->hqd', rounded, value_rows.astype(jnp.float32))
        return (mixed / totals[..., None]).astype(jnp.bfloat16)
    groups = jnp.repeat(jnp.arange(KVH, dtype=jnp.int32), block_count)
    blocks = jnp.tile(jnp.arange(block_count, dtype=jnp.int32), KVH)
    outputs = lax.map(one_item, (groups, blocks))
    attention = outputs.reshape(KVH, block_count, group_size, TOK_BLK, HD).transpose(1, 3, 0, 2, 4).reshape(total_tokens, H * HD)
    pages = jnp.stack([keys, values], axis=2).reshape(PAGES, PAGE, 2 * KVH * HD)
    kv_cache = jnp.zeros_like(pages).at[cache_slot].set(pages)
    return (attention, kv_cache)
```

```python
import math

import jax
import jax.numpy as jnp
from jax import lax
from jax.experimental import pallas as pl
from jax.experimental.pallas import tpu as pltpu
from jax.sharding import PartitionSpec as P

MESH = pl.DeviceIdType.MESH

D = 4096
H = 32
KVH = 4
HD = 128
PAGES_DEV = 16


epsilon = 1e-06
rope_base = 5000000.0
masked_out = -1e30


def token_places(prompt_lengths, token_index):
    prompt_ends = jnp.cumsum(prompt_lengths)
    prompt_starts = prompt_ends - prompt_lengths
    segment = jnp.sum((token_index[:, None] >= prompt_ends[None, :]).astype(jnp.int32), axis=1)
    chosen = segment[:, None] == jnp.arange(prompt_lengths.shape[0], dtype=jnp.int32)[None, :]
    opening = jnp.sum(jnp.where(chosen, prompt_starts[None, :], 0), axis=1)
    return (segment, token_index - opening)


def rotate(vectors, places):
    half_size = vectors.shape[-1] // 2
    frequency = rope_base ** (-(jnp.arange(half_size, dtype=jnp.float32) * 2.0) / vectors.shape[-1])
    angles = places.astype(jnp.float32)[:, None] * frequency[None, :]
    cos_part = jnp.cos(angles)[:, None, :]
    sin_part = jnp.sin(angles)[:, None, :]
    leading = vectors[..., :half_size]
    trailing = vectors[..., half_size:]
    return jnp.concatenate(
        [leading * cos_part - trailing * sin_part, trailing * cos_part + leading * sin_part],
        axis=-1,
    )


def local(hidden_in, norm_gain, query_proj, kv_proj, prompt_lengths, cache_slot):
    count_gx = lax.axis_size("gx")
    count_gy = lax.axis_size("gy")
    where_gx = lax.axis_index("gx")
    where_gy = lax.axis_index("gy")
    local_rows = hidden_in.shape[0]
    block_tokens = local_rows * count_gx // count_gy
    all_tokens = block_tokens * count_gy
    heads_here = query_proj.shape[0] // HD
    group_size = H // KVH
    share = count_gx // KVH
    kv_head = where_gx * heads_here // group_size
    contract = (((1,), (1,)), ((), ()))
    kv_width = 2 * HD
    kv_start = kv_head * 2 * HD
    kv_rows = lax.dynamic_slice_in_dim(kv_proj, kv_start, kv_width, 0)
    widened = hidden_in.astype(jnp.float32)
    squares = jnp.sum(widened * widened, axis=1)
    totals = lax.psum(squares, "gy")
    normed = (
        widened * lax.rsqrt(totals / D + epsilon)[:, None] * norm_gain.astype(jnp.float32)[None, :]
    ).astype(jnp.bfloat16)
    gathered = lax.all_gather(normed, "gx", axis=0, tiled=True)
    stacked = jnp.concatenate([query_proj, kv_rows], axis=0)
    projected = lax.psum_scatter(
        lax.dot_general(gathered, stacked, contract, preferred_element_type=jnp.float32),
        "gy",
        scatter_dimension=0,
        tiled=True,
    )
    every_index = jnp.arange(all_tokens, dtype=jnp.int32)
    segment_all, place_all = token_places(prompt_lengths, every_index)
    first_query = where_gy * block_tokens
    token_index = first_query + jnp.arange(block_tokens, dtype=jnp.int32)
    segment_own = lax.dynamic_slice_in_dim(segment_all, first_query, block_tokens, 0)
    place_own = lax.dynamic_slice_in_dim(place_all, first_query, block_tokens, 0)
    query_cols = heads_here * HD
    queries = rotate(
        projected[:, :query_cols].reshape(block_tokens, heads_here, HD), place_own
    ).astype(jnp.bfloat16)
    keys = rotate(projected[:, query_cols : query_cols + HD][:, None, :], place_own)[
        :, 0, :
    ].astype(jnp.bfloat16)
    values = projected[:, query_cols + HD :].astype(jnp.bfloat16)
    if share == 2:
        cache_cols = jnp.where(where_gx % 2 == 0, keys, values)
    else:
        cache_cols = jnp.concatenate([keys, values], axis=1)
    score_scale = 1.0 / math.sqrt(HD)
    last_query = first_query + block_tokens - 1
    first_segment = segment_own[0]
    initial = (
        jnp.full((heads_here, block_tokens), masked_out, jnp.float32),
        jnp.zeros((heads_here, block_tokens), jnp.float32),
        jnp.zeros((heads_here, block_tokens, HD), jnp.float32),
    )
    key_piece = lax.all_gather(keys, "gy", axis=0, tiled=True)
    value_piece = lax.all_gather(values, "gy", axis=0, tiled=True)
    block_count = key_piece.shape[0] // block_tokens
    key_blocks = key_piece.reshape(block_count, block_tokens, HD)
    value_blocks = value_piece.reshape(block_count, block_tokens, HD)

    def one_block(current, inputs):
        key_rows, value_rows, offset = inputs
        block_begin = offset * block_tokens
        key_segment = lax.dynamic_slice_in_dim(segment_all, block_begin, block_tokens, 0)
        skipped = jnp.logical_or(
            block_begin > last_query, key_segment[block_tokens - 1] < first_segment
        )

        def compute(previous):
            running_max, running_sum, running_acc = previous
            key_index = block_begin + jnp.arange(block_tokens, dtype=jnp.int32)
            allowed = (key_segment[None, :] == segment_own[:, None]) & (
                key_index[None, :] <= token_index[:, None]
            )
            scores = (
                jnp.einsum("qhd,kd->hqk", queries, key_rows, preferred_element_type=jnp.float32)
                * score_scale
            )
            scores = jnp.where(allowed[None], scores, masked_out)
            new_max = jnp.maximum(running_max, jnp.max(scores, axis=2))
            weights = jnp.where(allowed[None], jnp.exp(scores - new_max[..., None]), 0.0)
            factor = jnp.exp(running_max - new_max)
            new_sum = running_sum * factor + jnp.sum(weights, axis=2)
            update = jnp.einsum(
                "hqk,kd->hqd",
                weights.astype(jnp.bfloat16),
                value_rows,
                preferred_element_type=jnp.float32,
            )
            return (new_max, new_sum, running_acc * factor[..., None] + update)

        return (lax.cond(skipped, lambda previous: previous, compute, current), None)

    offsets = jnp.arange(block_count, dtype=jnp.int32)
    result, unused = lax.scan(one_block, initial, (key_blocks, value_blocks, offsets))
    final_max, final_sum, final_acc = result
    attention = (
        (final_acc / final_sum[..., None])
        .transpose(1, 0, 2)
        .reshape(block_tokens, query_cols)
        .astype(jnp.bfloat16)
    )
    pages_dev = PAGES_DEV
    page_len = block_tokens // pages_dev
    width_cols = cache_cols.shape[1]
    my_pages = cache_cols.reshape(pages_dev, page_len * width_cols)
    capacity = max(1, pages_dev // count_gy)
    slots_all = count_gy * capacity
    owners = (cache_slot // pages_dev).reshape(count_gy, pages_dev)
    page_range = jnp.arange(pages_dev, dtype=jnp.int32)
    earlier = page_range[None, :] < page_range[:, None]
    same_owner = owners[:, :, None] == owners[:, None, :]
    ranks = jnp.sum((same_owner & earlier[None]).astype(jnp.int32), axis=2)
    my_owner = lax.dynamic_index_in_dim(owners, where_gy, 0, keepdims=False)
    my_rank = lax.dynamic_index_in_dim(ranks, where_gy, 0, keepdims=False)
    target = my_owner * capacity + my_rank
    slot_range = jnp.arange(slots_all, dtype=jnp.int32)
    send_map = (slot_range[:, None] == target[None, :]).astype(jnp.bfloat16)
    outgoing = jnp.dot(send_map, my_pages, preferred_element_type=jnp.float32).astype(jnp.bfloat16)
    outgoing = outgoing.reshape(count_gy, capacity * page_len * width_cols)
    incoming = lax.all_to_all(outgoing, "gy", split_axis=0, concat_axis=0, tiled=True)
    wanted = where_gy * pages_dev + page_range
    matches = cache_slot[None, :] == wanted[:, None]
    page_ids = jnp.arange(cache_slot.shape[0], dtype=jnp.int32)
    source_page = jnp.sum(jnp.where(matches, page_ids[None, :], 0), axis=1)
    source_rank = jnp.sum(jnp.where(matches, ranks.reshape(-1)[None, :], 0), axis=1)
    source_slot = source_page // pages_dev * capacity + source_rank
    take_map = (source_slot[:, None] == slot_range[None, :]).astype(jnp.bfloat16)
    cache_block = jnp.dot(
        take_map,
        incoming.reshape(slots_all, page_len * width_cols),
        preferred_element_type=jnp.float32,
    )
    cache_block = cache_block.astype(jnp.bfloat16).reshape(pages_dev, page_len, width_cols)
    return (attention, cache_block)


BLK = 256
TWO_PI_PARTS = (6.28125, 4059.0 / 2**21, 2.0 * math.pi - 6.28125 - 4059.0 / 2**21)


def fused_kernel(
    lengths_ref, place_ref, hid_ref, gain_ref, freq_ref, wq_ref, wkv_ref,
    out_ref, cache_ref,
    squares, inverse, gain_other, x_own, x_other, w_other, normed, part, final,
    up_out, up_in, down_out, down_in, kv_all, bias, cos_ref, sin_ref,
    sq_send, sq_recv, inv_send, inv_recv, gain_sem, x_send, xo_recv, xn_recv,
    w_send, w_recv, up_send, up_recv, down_send, down_recv, kz_send, ky_send, kv_recv,
):
    gx = lax.axis_index("gx")
    gy = lax.axis_index("gy")
    y = lax.rem(gy, 2)
    z = lax.div(gy, 2)
    core_peer = gx + 1 - 2 * lax.rem(gx, 2)
    x_peer = lax.rem(gx + 2, 4)
    far_peer = 3 - gx
    y_peer = gy + 1 - 2 * y
    depth = hid_ref.shape[1]
    chunks = w_other.shape[0]

    def remote(src, dst, send_sem, recv_sem, to_gx, to_gy):
        return pltpu.make_async_remote_copy(
            src_ref=src, dst_ref=dst, send_sem=send_sem, recv_sem=recv_sem,
            device_id=(to_gx, to_gy), device_id_type=MESH,
        )

    barrier = pltpu.get_barrier_semaphore()
    for step in range(1, 8):
        pl.semaphore_signal(barrier, inc=1, device_id=(gx, lax.rem(gy + step, 8)), device_id_type=MESH)
    for step in range(1, 4):
        pl.semaphore_signal(barrier, inc=1, device_id=(lax.rem(gx + step, 4), gy), device_id_type=MESH)

    widened = hid_ref[...].astype(jnp.float32)
    squares[gy] = lax.dot_general(
        jnp.ones((8, depth), jnp.float32), widened * widened, (((1,), (1,)), ((), ())),
        precision=lax.Precision.HIGHEST, preferred_element_type=jnp.float32,
    )
    own_rows = pl.ds(pl.multiple_of(y * BLK, BLK), BLK)
    other_rows = pl.ds(pl.multiple_of((1 - y) * BLK, BLK), BLK)
    x_own[gx] = hid_ref[own_rows, :]
    pl.semaphore_wait(barrier, 10)

    sends = []

    def go(copy):
        copy.start()
        sends.append(copy)

    for step in range(1, 8):
        go(remote(squares.at[gy], squares.at[gy], sq_send.at[step], sq_recv.at[gy], gx, lax.rem(gy + step, 8)))
    go(remote(gain_ref, gain_other, gain_sem.at[0], gain_sem.at[1], gx, y_peer))
    go(remote(hid_ref.at[other_rows, :], x_other.at[gx], x_send.at[0], xn_recv.at[gx], gx, y_peer))
    go(remote(hid_ref.at[own_rows, :], x_own.at[gx], x_send.at[1], xo_recv.at[gx], x_peer, gy))
    go(remote(hid_ref.at[own_rows, :], x_own.at[gx], x_send.at[2], xo_recv.at[gx], core_peer, gy))
    kv_rows = pl.ds(pl.multiple_of(gx * 2 * HD, 2 * HD), 2 * HD)
    go(remote(wkv_ref.at[kv_rows, :], w_other.at[0], w_send.at[0], w_recv.at[0], gx, y_peer))
    for c in range(1, chunks):
        go(remote(wq_ref.at[pl.ds((c - 1) * BLK, BLK), :], w_other.at[c], w_send.at[c], w_recv.at[c], gx, y_peer))

    def arrived(dst, recv_sem):
        remote(dst, dst, x_send.at[0], recv_sem, gx, y_peer).wait_recv()

    first_token = gy * BLK
    token = first_token + lax.broadcasted_iota(jnp.int32, (BLK, HD), 0)
    opening = jnp.zeros((BLK, HD), jnp.int32)
    end = jnp.zeros((1, HD), jnp.int32)
    for s in range(lengths_ref.shape[0]):
        end = end + lengths_ref[s : s + 1, :]
        opening = jnp.where(token >= end, end, opening)
    angles = (token - opening).astype(jnp.float32) * freq_ref[0:1, :]
    turns = jnp.floor(angles * (0.5 / math.pi) + 0.5)
    for piece in TWO_PI_PARTS:
        angles = angles - turns * piece
    cos_ref[...] = jnp.cos(angles)
    sign = jnp.where(lax.broadcasted_iota(jnp.int32, (BLK, HD), 1) < HD // 2, -1.0, 1.0)
    sin_ref[...] = jnp.sin(angles) * sign
    window = bias.shape[1] // BLK
    start_block = jnp.maximum(gy - (window - 1), 0)
    for s in range(window):
        for half in range(2):
            lanes = s * BLK + half * HD
            key = start_block * BLK + lanes + lax.broadcasted_iota(jnp.int32, (BLK, HD), 1)
            bias[:, lanes : lanes + HD] = jnp.where((key >= opening) & (key <= token), 0.0, masked_out)

    for step in range(1, 8):
        source = lax.rem(gy + step, 8)
        arrived(squares.at[source], sq_recv.at[source])
    total = squares[0]
    for s in range(1, 8):
        total = total + squares[s]
    inverse[gx] = lax.rsqrt(total / D + epsilon)
    for step in range(1, 4):
        go(remote(inverse.at[gx], inverse.at[gx], inv_send.at[step], inv_recv.at[gx], lax.rem(gx + step, 4), gy))

    arrived(x_other.at[gx], xn_recv.at[gx])
    go(remote(x_other.at[gx], x_other.at[gx], x_send.at[3], xn_recv.at[gx], x_peer, gy))
    go(remote(x_other.at[gx], x_other.at[gx], x_send.at[4], xn_recv.at[gx], core_peer, gy))
    arrived(x_own.at[x_peer], xo_recv.at[x_peer])
    go(remote(x_own.at[x_peer], x_own.at[x_peer], x_send.at[5], xo_recv.at[x_peer], core_peer, gy))
    arrived(x_other.at[x_peer], xn_recv.at[x_peer])
    go(remote(x_other.at[x_peer], x_other.at[x_peer], x_send.at[6], xn_recv.at[x_peer], core_peer, gy))
    arrived(gain_other, gain_sem.at[1])
    for step in range(1, 4):
        source = lax.rem(gx + step, 4)
        arrived(inverse.at[source], inv_recv.at[source])
    for peer in (core_peer, far_peer):
        arrived(x_own.at[peer], xo_recv.at[peer])
        arrived(x_other.at[peer], xn_recv.at[peer])

    eighth = jnp.full((8, depth), 0.125, jnp.float32)

    def normalise(m, carry):
        scale = lax.dot_general(
            inverse[m, :, own_rows], eighth, (((0,), (0,)), ((), ())),
            precision=lax.Precision.HIGHEST, preferred_element_type=jnp.float32,
        )
        normed[m, :, 0:depth] = (x_own[m].astype(jnp.float32) * scale * gain_ref[0:1, :]).astype(jnp.bfloat16)
        normed[m, :, depth:] = (x_other[m].astype(jnp.float32) * scale * gain_other[0:1, :]).astype(jnp.bfloat16)
        return carry

    lax.fori_loop(0, 4, normalise, 0)

    contract = (((1,), (1,)), ((), ()))

    def multiply(c, w_here):
        arrived(w_other.at[c], w_recv.at[c])

        def one(m, carry):
            part[m] = lax.dot_general(
                normed[m, :, 0:depth], w_here(), contract, preferred_element_type=jnp.float32
            ) + lax.dot_general(
                normed[m, :, depth:], w_other[c], contract, preferred_element_type=jnp.float32
            )
            return carry

        lax.fori_loop(0, 4, one, 0)
        final[c] = part[z]

    def up_copy(c, t):
        return remote(up_out.at[c, t], up_in.at[c, t], up_send.at[c, t], up_recv.at[c, t], gx, gy + 2)

    def down_copy(c, t):
        return remote(down_out.at[c, t], down_in.at[c, t], down_send.at[c, t], down_recv.at[c, t], gx, gy - 2)

    def pass_on(c):
        for t in (3, 2, 1):
            @pl.when(z == 0)
            def _():
                up_out[c, t] = part[t].astype(jnp.bfloat16)
                up_copy(c, t).start()

            @pl.when((z > 0) & (z < t))
            def _():
                arrived(up_in.at[c, t], up_recv.at[c, t])
                up_out[c, t] = (part[t] + up_in[c, t].astype(jnp.float32)).astype(jnp.bfloat16)
                up_copy(c, t).start()

            d = 3 - t

            @pl.when(z == 3)
            def _():
                down_out[c, d] = part[d].astype(jnp.bfloat16)
                down_copy(c, d).start()

            @pl.when((z < 3) & (z > d))
            def _():
                arrived(down_in.at[c, d], down_recv.at[c, d])
                down_out[c, d] = (part[d] + down_in[c, d].astype(jnp.float32)).astype(jnp.bfloat16)
                down_copy(c, d).start()

    def finish(c):
        @pl.when(z > 0)
        def _():
            arrived(up_in.at[c, z], up_recv.at[c, z])
            final[c] = final[c] + up_in[c, z].astype(jnp.float32)

        @pl.when(z < 3)
        def _():
            arrived(down_in.at[c, z], down_recv.at[c, z])
            final[c] = final[c] + down_in[c, z].astype(jnp.float32)

    def rotated(u):
        return (u * cos_ref[...] + pltpu.roll(u, HD // 2, 1) * sin_ref[...]).astype(jnp.bfloat16)

    def q_chunk(c):
        rows = pl.ds(pl.multiple_of((c - 1) * BLK, BLK), BLK)
        multiply(c, lambda: wq_ref[rows, :])
        pass_on(c)

    multiply(0, lambda: wkv_ref[kv_rows, :])
    pass_on(0)
    q_chunk(1)

    finish(0)
    kv_all[gy, :, 0:HD] = rotated(final[0, :, 0:HD])
    kv_all[gy, :, HD:] = final[0, :, HD:].astype(jnp.bfloat16)
    for step in range(1, 4):
        go(remote(kv_all.at[gy], kv_all.at[gy], kz_send.at[step], kv_recv.at[gy], gx, lax.rem(gy + 2 * step, 8)))
    go(remote(kv_all.at[gy], kv_all.at[gy], ky_send.at[0], kv_recv.at[gy], gx, y_peer))
    q_chunk(2)
    for step in range(1, 4):
        source = lax.rem(gy + 2 * step, 8)
        arrived(kv_all.at[source], kv_recv.at[source])
        go(remote(kv_all.at[source], kv_all.at[source], ky_send.at[step], kv_recv.at[source], gx, y_peer))

    def late_chunk(c, carry):
        q_chunk(c)
        return carry

    lax.fori_loop(3, chunks, late_chunk, 0)
    for step in range(4):
        source = lax.rem(y_peer + 2 * step, 8)
        arrived(kv_all.at[source], kv_recv.at[source])

    score_scale = 1.0 / math.sqrt(HD)
    keys = pl.ds(start_block, window)

    def attend(c, carry):
        finish(c)
        for half in range(2):
            query = rotated(final[c, :, half * HD : (half + 1) * HD])
            key_rows = kv_all[keys, :, 0:HD].reshape(window * BLK, HD)
            value_rows = kv_all[keys, :, HD:].reshape(window * BLK, HD)
            scores = lax.dot_general(query, key_rows, contract, preferred_element_type=jnp.float32)
            scores = scores * score_scale + bias[...]
            weights = jnp.exp(scores - jnp.max(scores, axis=1, keepdims=True))
            sums = jnp.sum(weights, axis=1, keepdims=True)
            mixed = jnp.dot(weights.astype(jnp.bfloat16), value_rows, preferred_element_type=jnp.float32)
            column = pl.multiple_of((c - 1) * BLK + half * HD, HD)
            out_ref[:, pl.ds(column, HD)] = (mixed / sums).astype(jnp.bfloat16)
        return carry

    lax.fori_loop(1, chunks, attend, 0)

    wanted = gy * BLK + lax.broadcasted_iota(jnp.int32, (BLK, BLK), 0)
    picked = jnp.zeros((BLK, 2 * HD), jnp.float32)
    for s in range(8):
        chosen = jnp.where(place_ref[:, s * BLK : (s + 1) * BLK] == wanted, 1.0, 0.0).astype(jnp.bfloat16)
        picked = picked + jnp.dot(chosen, kv_all[s], preferred_element_type=jnp.float32)
    cache_ref[...] = picked.astype(jnp.bfloat16).reshape(cache_ref.shape)

    for copy in sends:
        copy.wait_send()

    def drain(c, carry):
        for t in (3, 2, 1):
            @pl.when(z < t)
            def _():
                up_copy(c, t).wait_send()

            @pl.when(z > 3 - t)
            def _():
                down_copy(c, 3 - t).wait_send()
        return carry

    lax.fori_loop(0, chunks, drain, 0)


def fused(hidden_in, norm_gain, query_proj, kv_proj, prompt_lengths, cache_slot):
    width = hidden_in.shape[1]
    query_cols = query_proj.shape[0]
    chunks = 1 + query_cols // BLK
    page_len = BLK // PAGES_DEV
    places = (
        cache_slot[:, None] * page_len + jnp.arange(page_len, dtype=jnp.int32)[None, :]
    ).reshape(1, -1)
    lengths = jnp.broadcast_to(prompt_lengths[:, None], (prompt_lengths.shape[0], HD))
    gain = jnp.broadcast_to(norm_gain.astype(jnp.float32)[None, :], (8, width))
    half_size = HD // 2
    frequency = rope_base ** (-(jnp.arange(half_size, dtype=jnp.float32) * 2.0) / HD)
    frequency = jnp.broadcast_to(jnp.concatenate([frequency, frequency])[None, :], (8, HD))
    all_tokens = hidden_in.shape[0] * lax.axis_size("gx")
    window = all_tokens // 2 // BLK + 1
    bf16, f32 = jnp.bfloat16, jnp.float32
    dma = pltpu.SemaphoreType.DMA
    vmem = pl.BlockSpec(memory_space=pltpu.VMEM)
    return pl.pallas_call(
        fused_kernel,
        out_shape=(
            jax.ShapeDtypeStruct((BLK, query_cols), bf16),
            jax.ShapeDtypeStruct((PAGES_DEV, page_len, 2 * HD), bf16),
        ),
        in_specs=[vmem] * 7,
        out_specs=(vmem, vmem),
        scratch_shapes=[
            pltpu.VMEM((8, 8, 2 * BLK), f32),
            pltpu.VMEM((4, 8, 2 * BLK), f32),
            pltpu.VMEM((8, width), f32),
            pltpu.VMEM((4, BLK, width), bf16),
            pltpu.VMEM((4, BLK, width), bf16),
            pltpu.VMEM((chunks, BLK, width), bf16),
            pltpu.VMEM((4, BLK, 2 * width), bf16),
            pltpu.VMEM((4, BLK, BLK), f32),
            pltpu.VMEM((chunks, BLK, BLK), f32),
            pltpu.VMEM((chunks, 4, BLK, BLK), bf16),
            pltpu.VMEM((chunks, 4, BLK, BLK), bf16),
            pltpu.VMEM((chunks, 4, BLK, BLK), bf16),
            pltpu.VMEM((chunks, 4, BLK, BLK), bf16),
            pltpu.VMEM((8, BLK, 2 * HD), bf16),
            pltpu.VMEM((BLK, window * BLK), f32),
            pltpu.VMEM((BLK, HD), f32),
            pltpu.VMEM((BLK, HD), f32),
            dma((8,)), dma((8,)), dma((4,)), dma((4,)), dma((2,)), dma((7,)), dma((4,)), dma((4,)),
            dma((chunks,)), dma((chunks,)), dma((chunks, 4)), dma((chunks, 4)), dma((chunks, 4)), dma((chunks, 4)),
            dma((4,)), dma((4,)), dma((8,)),
        ],
        compiler_params=pltpu.CompilerParams(
            collective_id=0, has_side_effects=True, vmem_limit_bytes=56 * 1024 * 1024
        ),
        cost_estimate=pl.CostEstimate(flops=4000000000, bytes_accessed=8000000, transcendentals=3000000),
    )(lengths, places, hidden_in, gain, frequency, query_proj, kv_proj)


def solution(mesh):
    form = fused if (mesh.shape["gx"], mesh.shape["gy"]) == (4, 8) else local
    return jax.shard_map(
        form,
        mesh=mesh,
        in_specs=(P("gx", "gy"), P("gy"), P("gx", "gy"), P(None, "gy"), P(), P()),
        out_specs=(P("gy", "gx"), P("gy", None, "gx")),
        check_vma=False,
    )
```

```python
import math

import jax
import jax.numpy as jnp
import numpy as np
from jax import lax
from jax.experimental import pallas as pl
from jax.experimental.pallas import tpu as pltpu
from jax.sharding import PartitionSpec as P

MESH = pl.DeviceIdType.MESH

D = 4096
H = 32
KVH = 4
HD = 128
PAGES_DEV = 16


epsilon = 1e-06
rope_base = 5000000.0
masked_out = -1e30


def token_places(prompt_lengths, token_index):
    prompt_ends = jnp.cumsum(prompt_lengths)
    prompt_starts = prompt_ends - prompt_lengths
    segment = jnp.sum((token_index[:, None] >= prompt_ends[None, :]).astype(jnp.int32), axis=1)
    chosen = segment[:, None] == jnp.arange(prompt_lengths.shape[0], dtype=jnp.int32)[None, :]
    opening = jnp.sum(jnp.where(chosen, prompt_starts[None, :], 0), axis=1)
    return (segment, token_index - opening)


def rotate(vectors, places):
    half_size = vectors.shape[-1] // 2
    frequency = rope_base ** (-(jnp.arange(half_size, dtype=jnp.float32) * 2.0) / vectors.shape[-1])
    angles = places.astype(jnp.float32)[:, None] * frequency[None, :]
    cos_part = jnp.cos(angles)[:, None, :]
    sin_part = jnp.sin(angles)[:, None, :]
    leading = vectors[..., :half_size]
    trailing = vectors[..., half_size:]
    return jnp.concatenate(
        [leading * cos_part - trailing * sin_part, trailing * cos_part + leading * sin_part],
        axis=-1,
    )


def local(hidden_in, norm_gain, query_proj, kv_proj, prompt_lengths, cache_slot):
    count_gx = lax.axis_size("gx")
    count_gy = lax.axis_size("gy")
    where_gx = lax.axis_index("gx")
    where_gy = lax.axis_index("gy")
    local_rows = hidden_in.shape[0]
    block_tokens = local_rows * count_gx // count_gy
    all_tokens = block_tokens * count_gy
    heads_here = query_proj.shape[0] // HD
    group_size = H // KVH
    share = count_gx // KVH
    kv_head = where_gx * heads_here // group_size
    contract = (((1,), (1,)), ((), ()))
    kv_width = 2 * HD
    kv_start = kv_head * 2 * HD
    kv_rows = lax.dynamic_slice_in_dim(kv_proj, kv_start, kv_width, 0)
    widened = hidden_in.astype(jnp.float32)
    squares = jnp.sum(widened * widened, axis=1)
    totals = lax.psum(squares, "gy")
    normed = (
        widened * lax.rsqrt(totals / D + epsilon)[:, None] * norm_gain.astype(jnp.float32)[None, :]
    ).astype(jnp.bfloat16)
    gathered = lax.all_gather(normed, "gx", axis=0, tiled=True)
    stacked = jnp.concatenate([query_proj, kv_rows], axis=0)
    projected = lax.psum_scatter(
        lax.dot_general(gathered, stacked, contract, preferred_element_type=jnp.float32),
        "gy",
        scatter_dimension=0,
        tiled=True,
    )
    every_index = jnp.arange(all_tokens, dtype=jnp.int32)
    segment_all, place_all = token_places(prompt_lengths, every_index)
    first_query = where_gy * block_tokens
    token_index = first_query + jnp.arange(block_tokens, dtype=jnp.int32)
    segment_own = lax.dynamic_slice_in_dim(segment_all, first_query, block_tokens, 0)
    place_own = lax.dynamic_slice_in_dim(place_all, first_query, block_tokens, 0)
    query_cols = heads_here * HD
    queries = rotate(
        projected[:, :query_cols].reshape(block_tokens, heads_here, HD), place_own
    ).astype(jnp.bfloat16)
    keys = rotate(projected[:, query_cols : query_cols + HD][:, None, :], place_own)[
        :, 0, :
    ].astype(jnp.bfloat16)
    values = projected[:, query_cols + HD :].astype(jnp.bfloat16)
    if share == 2:
        cache_cols = jnp.where(where_gx % 2 == 0, keys, values)
    else:
        cache_cols = jnp.concatenate([keys, values], axis=1)
    score_scale = 1.0 / math.sqrt(HD)
    last_query = first_query + block_tokens - 1
    first_segment = segment_own[0]
    initial = (
        jnp.full((heads_here, block_tokens), masked_out, jnp.float32),
        jnp.zeros((heads_here, block_tokens), jnp.float32),
        jnp.zeros((heads_here, block_tokens, HD), jnp.float32),
    )
    key_piece = lax.all_gather(keys, "gy", axis=0, tiled=True)
    value_piece = lax.all_gather(values, "gy", axis=0, tiled=True)
    block_count = key_piece.shape[0] // block_tokens
    key_blocks = key_piece.reshape(block_count, block_tokens, HD)
    value_blocks = value_piece.reshape(block_count, block_tokens, HD)

    def one_block(current, inputs):
        key_rows, value_rows, offset = inputs
        block_begin = offset * block_tokens
        key_segment = lax.dynamic_slice_in_dim(segment_all, block_begin, block_tokens, 0)
        skipped = jnp.logical_or(
            block_begin > last_query, key_segment[block_tokens - 1] < first_segment
        )

        def compute(previous):
            running_max, running_sum, running_acc = previous
            key_index = block_begin + jnp.arange(block_tokens, dtype=jnp.int32)
            allowed = (key_segment[None, :] == segment_own[:, None]) & (
                key_index[None, :] <= token_index[:, None]
            )
            scores = (
                jnp.einsum("qhd,kd->hqk", queries, key_rows, preferred_element_type=jnp.float32)
                * score_scale
            )
            scores = jnp.where(allowed[None], scores, masked_out)
            new_max = jnp.maximum(running_max, jnp.max(scores, axis=2))
            weights = jnp.where(allowed[None], jnp.exp(scores - new_max[..., None]), 0.0)
            factor = jnp.exp(running_max - new_max)
            new_sum = running_sum * factor + jnp.sum(weights, axis=2)
            update = jnp.einsum(
                "hqk,kd->hqd",
                weights.astype(jnp.bfloat16),
                value_rows,
                preferred_element_type=jnp.float32,
            )
            return (new_max, new_sum, running_acc * factor[..., None] + update)

        return (lax.cond(skipped, lambda previous: previous, compute, current), None)

    offsets = jnp.arange(block_count, dtype=jnp.int32)
    result, unused = lax.scan(one_block, initial, (key_blocks, value_blocks, offsets))
    final_max, final_sum, final_acc = result
    attention = (
        (final_acc / final_sum[..., None])
        .transpose(1, 0, 2)
        .reshape(block_tokens, query_cols)
        .astype(jnp.bfloat16)
    )
    pages_dev = PAGES_DEV
    page_len = block_tokens // pages_dev
    width_cols = cache_cols.shape[1]
    my_pages = cache_cols.reshape(pages_dev, page_len * width_cols)
    capacity = max(1, pages_dev // count_gy)
    slots_all = count_gy * capacity
    owners = (cache_slot // pages_dev).reshape(count_gy, pages_dev)
    page_range = jnp.arange(pages_dev, dtype=jnp.int32)
    earlier = page_range[None, :] < page_range[:, None]
    same_owner = owners[:, :, None] == owners[:, None, :]
    ranks = jnp.sum((same_owner & earlier[None]).astype(jnp.int32), axis=2)
    my_owner = lax.dynamic_index_in_dim(owners, where_gy, 0, keepdims=False)
    my_rank = lax.dynamic_index_in_dim(ranks, where_gy, 0, keepdims=False)
    target = my_owner * capacity + my_rank
    slot_range = jnp.arange(slots_all, dtype=jnp.int32)
    send_map = (slot_range[:, None] == target[None, :]).astype(jnp.bfloat16)
    outgoing = jnp.dot(send_map, my_pages, preferred_element_type=jnp.float32).astype(jnp.bfloat16)
    outgoing = outgoing.reshape(count_gy, capacity * page_len * width_cols)
    incoming = lax.all_to_all(outgoing, "gy", split_axis=0, concat_axis=0, tiled=True)
    wanted = where_gy * pages_dev + page_range
    matches = cache_slot[None, :] == wanted[:, None]
    page_ids = jnp.arange(cache_slot.shape[0], dtype=jnp.int32)
    source_page = jnp.sum(jnp.where(matches, page_ids[None, :], 0), axis=1)
    source_rank = jnp.sum(jnp.where(matches, ranks.reshape(-1)[None, :], 0), axis=1)
    source_slot = source_page // pages_dev * capacity + source_rank
    take_map = (source_slot[:, None] == slot_range[None, :]).astype(jnp.bfloat16)
    cache_block = jnp.dot(
        take_map,
        incoming.reshape(slots_all, page_len * width_cols),
        preferred_element_type=jnp.float32,
    )
    cache_block = cache_block.astype(jnp.bfloat16).reshape(pages_dev, page_len, width_cols)
    return (attention, cache_block)


BLK = 256
TWO_PI_PARTS = (6.28125, 4059.0 / 2**21, 2.0 * math.pi - 6.28125 - 4059.0 / 2**21)


def fused_kernel(
    lengths_ref, slot_ref, hid_ref, gain_row, freq_ref, wq_ref, wkv_ref,
    out_ref, cache_ref,
    squares, inverse, gain_ref, gain_other, x_own, x_other, w_other, normed, part, final,
    up_out, up_in, down_out, down_in, kv_all, bias, cos_ref, sin_ref,
    sq_send, sq_recv, inv_send, inv_recv, gain_sem, x_send, xo_recv, xn_recv,
    w_send, w_recv, up_send, up_recv, down_send, down_recv, kz_send, ky_send, kv_recv,
):
    gx = lax.axis_index("gx")
    gy = lax.axis_index("gy")
    y = lax.rem(gy, 2)
    z = lax.div(gy, 2)
    core_peer = gx + 1 - 2 * lax.rem(gx, 2)
    x_peer = lax.rem(gx + 2, 4)
    far_peer = 3 - gx
    y_peer = gy + 1 - 2 * y
    depth = hid_ref.shape[1]
    chunks = w_other.shape[0]

    def remote(src, dst, send_sem, recv_sem, to_gx, to_gy):
        return pltpu.make_async_remote_copy(
            src_ref=src, dst_ref=dst, send_sem=send_sem, recv_sem=recv_sem,
            device_id=(to_gx, to_gy), device_id_type=MESH,
        )

    barrier = pltpu.get_barrier_semaphore()
    for step in range(1, 8):
        pl.semaphore_signal(barrier, inc=1, device_id=(gx, lax.rem(gy + step, 8)), device_id_type=MESH)
    for step in range(1, 4):
        pl.semaphore_signal(barrier, inc=1, device_id=(lax.rem(gx + step, 4), gy), device_id_type=MESH)

    widened = hid_ref[...].astype(jnp.float32)
    squares[gy] = lax.dot_general(
        jnp.ones((8, depth), jnp.float32), widened * widened, (((1,), (1,)), ((), ())),
        precision=lax.Precision.HIGHEST, preferred_element_type=jnp.float32,
    )
    own_rows = pl.ds(pl.multiple_of(y * BLK, BLK), BLK)
    other_rows = pl.ds(pl.multiple_of((1 - y) * BLK, BLK), BLK)
    x_own[gx] = hid_ref[own_rows, :]
    gain_ref[...] = jnp.broadcast_to(gain_row[...].astype(jnp.float32), gain_ref.shape)
    pl.semaphore_wait(barrier, 10)

    sends = []

    def go(copy):
        copy.start()
        sends.append(copy)

    for step in range(1, 8):
        go(remote(squares.at[gy], squares.at[gy], sq_send.at[step], sq_recv.at[gy], gx, lax.rem(gy + step, 8)))
    go(remote(gain_ref, gain_other, gain_sem.at[0], gain_sem.at[1], gx, y_peer))
    go(remote(hid_ref.at[other_rows, :], x_other.at[gx], x_send.at[0], xn_recv.at[gx], gx, y_peer))
    go(remote(hid_ref.at[own_rows, :], x_own.at[gx], x_send.at[1], xo_recv.at[gx], x_peer, gy))
    go(remote(hid_ref.at[own_rows, :], x_own.at[gx], x_send.at[2], xo_recv.at[gx], core_peer, gy))
    kv_rows = pl.ds(pl.multiple_of(gx * 2 * HD, 2 * HD), 2 * HD)

    def send_weights(c):
        rows = wkv_ref.at[kv_rows, :] if c == 0 else wq_ref.at[pl.ds((c - 1) * BLK, BLK), :]
        go(remote(rows, w_other.at[c], w_send.at[c], w_recv.at[c], gx, y_peer))

    def arrived(dst, recv_sem):
        remote(dst, dst, x_send.at[0], recv_sem, gx, y_peer).wait_recv()

    first_token = gy * BLK
    token = first_token + lax.broadcasted_iota(jnp.int32, (BLK, HD), 0)
    opening = jnp.zeros((BLK, HD), jnp.int32)
    end = jnp.zeros((1, HD), jnp.int32)
    for s in range(lengths_ref.shape[1]):
        end = end + lengths_ref[0:1, s : s + 1]
        opening = jnp.where(token >= end, end, opening)
    angles = (token - opening).astype(jnp.float32) * freq_ref[0:1, :]
    turns = jnp.floor(angles * (0.5 / math.pi) + 0.5)
    for piece in TWO_PI_PARTS:
        angles = angles - turns * piece
    cos_ref[...] = jnp.cos(angles)
    sign = jnp.where(lax.broadcasted_iota(jnp.int32, (BLK, HD), 1) < HD // 2, -1.0, 1.0)
    sin_ref[...] = jnp.sin(angles) * sign
    window = bias.shape[1] // BLK
    start_block = jnp.maximum(gy - (window - 1), 0)
    for s in range(window):
        for half in range(2):
            lanes = s * BLK + half * HD
            key = start_block * BLK + lanes + lax.broadcasted_iota(jnp.int32, (BLK, HD), 1)
            bias[:, lanes : lanes + HD] = jnp.where((key >= opening) & (key <= token), 0.0, masked_out)

    for step in range(1, 8):
        source = lax.rem(gy + step, 8)
        arrived(squares.at[source], sq_recv.at[source])
    total = squares[0]
    for s in range(1, 8):
        total = total + squares[s]
    inverse[gx] = lax.rsqrt(total / D + epsilon)
    for step in range(1, 4):
        go(remote(inverse.at[gx], inverse.at[gx], inv_send.at[step], inv_recv.at[gx], lax.rem(gx + step, 4), gy))

    eighth = jnp.full((8, depth), 0.125, jnp.float32)

    def normalise(m):
        scale = lax.dot_general(
            inverse[m, :, own_rows], eighth, (((0,), (0,)), ((), ())),
            precision=lax.Precision.HIGHEST, preferred_element_type=jnp.float32,
        )
        normed[m, :, 0:depth] = (x_own[m].astype(jnp.float32) * scale * gain_ref[0:1, :]).astype(jnp.bfloat16)
        normed[m, :, depth:] = (x_other[m].astype(jnp.float32) * scale * gain_other[0:1, :]).astype(jnp.bfloat16)

    arrived(x_other.at[gx], xn_recv.at[gx])
    go(remote(x_other.at[gx], x_other.at[gx], x_send.at[3], xn_recv.at[gx], x_peer, gy))
    go(remote(x_other.at[gx], x_other.at[gx], x_send.at[4], xn_recv.at[gx], core_peer, gy))
    send_weights(0)
    arrived(x_own.at[x_peer], xo_recv.at[x_peer])
    go(remote(x_own.at[x_peer], x_own.at[x_peer], x_send.at[5], xo_recv.at[x_peer], core_peer, gy))
    arrived(gain_other, gain_sem.at[1])
    normalise(gx)
    arrived(x_own.at[core_peer], xo_recv.at[core_peer])
    arrived(x_other.at[core_peer], xn_recv.at[core_peer])
    arrived(inverse.at[core_peer], inv_recv.at[core_peer])
    normalise(core_peer)
    arrived(x_other.at[x_peer], xn_recv.at[x_peer])
    go(remote(x_other.at[x_peer], x_other.at[x_peer], x_send.at[6], xn_recv.at[x_peer], core_peer, gy))
    send_weights(1)
    arrived(inverse.at[x_peer], inv_recv.at[x_peer])
    normalise(x_peer)
    arrived(inverse.at[far_peer], inv_recv.at[far_peer])
    arrived(x_own.at[far_peer], xo_recv.at[far_peer])
    arrived(x_other.at[far_peer], xn_recv.at[far_peer])
    normalise(far_peer)

    contract = (((1,), (1,)), ((), ()))

    def multiply(c, w_here):
        arrived(w_other.at[c], w_recv.at[c])
        if isinstance(c, int) and c + 2 < chunks:
            send_weights(c + 2)

        def one(m, carry):
            part[m] = lax.dot_general(
                normed[m, :, 0:depth], w_here(), contract, preferred_element_type=jnp.float32
            ) + lax.dot_general(
                normed[m, :, depth:], w_other[c], contract, preferred_element_type=jnp.float32
            )
            return carry

        lax.fori_loop(0, 4, one, 0)
        final[c] = part[z]

    def up_copy(c, t):
        return remote(up_out.at[c, t], up_in.at[c, t], up_send.at[c, t], up_recv.at[c, t], gx, gy + 2)

    def down_copy(c, t):
        return remote(down_out.at[c, t], down_in.at[c, t], down_send.at[c, t], down_recv.at[c, t], gx, gy - 2)

    def pass_on(c, first=False):
        for t in (3, 2, 1):
            @pl.when(z == 0)
            def _():
                if t == 1:
                    up_copy(c, 3).wait_send()
                elif not first:
                    up_copy(c - 1, t - 1).wait_send()
                up_out[c, t] = part[t].astype(jnp.bfloat16)
                up_copy(c, t).start()

            @pl.when((z > 0) & (z < t))
            def _():
                arrived(up_in.at[c, t], up_recv.at[c, t])
                up_out[c, t] = (part[t] + up_in[c, t].astype(jnp.float32)).astype(jnp.bfloat16)
                up_copy(c, t).start()

            d = 3 - t

            @pl.when(z == 3)
            def _():
                if t == 1:
                    down_copy(c, 0).wait_send()
                elif not first:
                    down_copy(c - 1, d + 1).wait_send()
                down_out[c, d] = part[d].astype(jnp.bfloat16)
                down_copy(c, d).start()

            @pl.when((z < 3) & (z > d))
            def _():
                arrived(down_in.at[c, d], down_recv.at[c, d])
                down_out[c, d] = (part[d] + down_in[c, d].astype(jnp.float32)).astype(jnp.bfloat16)
                down_copy(c, d).start()

    def finish(c):
        @pl.when(z > 0)
        def _():
            arrived(up_in.at[c, z], up_recv.at[c, z])
            final[c] = final[c] + up_in[c, z].astype(jnp.float32)

        @pl.when(z < 3)
        def _():
            arrived(down_in.at[c, z], down_recv.at[c, z])
            final[c] = final[c] + down_in[c, z].astype(jnp.float32)

    def rotated(u):
        return (u * cos_ref[...] + pltpu.roll(u, HD // 2, 1) * sin_ref[...]).astype(jnp.bfloat16)

    def q_chunk(c):
        rows = pl.ds(pl.multiple_of((c - 1) * BLK, BLK), BLK)
        multiply(c, lambda: wq_ref[rows, :])
        pass_on(c)

    multiply(0, lambda: wkv_ref[kv_rows, :])
    pass_on(0, True)
    q_chunk(1)

    finish(0)
    kv_all[gy, :, 0:HD] = rotated(final[0, :, 0:HD])
    kv_all[gy, :, HD:] = final[0, :, HD:].astype(jnp.bfloat16)

    def kv_up(step):
        block = kv_all.at[gy - 2 * step]
        return remote(block, block, kz_send.at[0, step], kv_recv.at[gy - 2 * step], gx, gy + 2)

    def kv_down(step):
        block = kv_all.at[gy + 2 * step]
        return remote(block, block, kz_send.at[1, step], kv_recv.at[gy + 2 * step], gx, gy - 2)

    def kv_across(source, side, step):
        return remote(kv_all.at[source], kv_all.at[source], ky_send.at[side, step], kv_recv.at[source], gx, y_peer)

    def kv_step(step, act):
        @pl.when((z >= step) & (z < 3))
        def _():
            act(kv_up(step))

        @pl.when((z + step <= 3) & (z > 0))
        def _():
            act(kv_down(step))

        if step == 0:
            act(kv_across(gy, 0, 0))
        else:
            @pl.when(z >= step)
            def _():
                act(kv_across(gy - 2 * step, 0, step))

            @pl.when(z + step <= 3)
            def _():
                act(kv_across(gy + 2 * step, 1, step))

    def kv_forward(step):
        @pl.when(z >= step)
        def _():
            arrived(kv_all.at[gy - 2 * step], kv_recv.at[gy - 2 * step])

        @pl.when(z + step <= 3)
        def _():
            arrived(kv_all.at[gy + 2 * step], kv_recv.at[gy + 2 * step])

        kv_step(step, lambda copy: copy.start())

    kv_step(0, lambda copy: copy.start())
    q_chunk(2)
    kv_forward(1)
    q_chunk(3)
    kv_forward(2)
    q_chunk(4)
    kv_forward(3)
    for step in range(4):
        source = lax.rem(y_peer + 2 * step, 8)
        arrived(kv_all.at[source], kv_recv.at[source])

    score_scale = 1.0 / math.sqrt(HD)
    keys = pl.ds(start_block, window)

    def attend(c, carry):
        finish(c)
        for half in range(2):
            query = rotated(final[c, :, half * HD : (half + 1) * HD])
            key_rows = kv_all[keys, :, 0:HD].reshape(window * BLK, HD)
            value_rows = kv_all[keys, :, HD:].reshape(window * BLK, HD)
            scores = lax.dot_general(query, key_rows, contract, preferred_element_type=jnp.float32)
            scores = scores * score_scale + bias[...]
            weights = jnp.exp(scores - jnp.max(scores, axis=1, keepdims=True))
            sums = jnp.sum(weights, axis=1, keepdims=True)
            mixed = jnp.dot(weights.astype(jnp.bfloat16), value_rows, preferred_element_type=jnp.float32)
            column = pl.multiple_of((c - 1) * BLK + half * HD, HD)
            out_ref[:, pl.ds(column, HD)] = (mixed / sums).astype(jnp.bfloat16)
        return carry

    lax.fori_loop(1, chunks, attend, 0)

    page_len = cache_ref.shape[1]
    pages = slot_ref.shape[1]
    wanted = (gy * BLK + lax.broadcasted_iota(jnp.int32, (BLK, BLK), 0)).astype(jnp.float32)
    page = lax.broadcasted_iota(jnp.int32, (pages, BLK), 0)
    lane = lax.broadcasted_iota(jnp.int32, (pages, BLK), 1)
    offset = lax.rem(lane[0:8, :], page_len).astype(jnp.float32)
    slots = jnp.broadcast_to(slot_ref[...].astype(jnp.float32), (8, pages)).astype(jnp.bfloat16)
    picked = jnp.zeros((BLK, 2 * HD), jnp.float32)
    for s in range(8):
        spread = jnp.where(page == s * PAGES_DEV + lax.div(lane, page_len), 1.0, 0.0).astype(jnp.bfloat16)
        places = jnp.dot(slots, spread, preferred_element_type=jnp.float32) * page_len + offset
        chosen = jnp.where(places[0:1, :] == wanted, 1.0, 0.0).astype(jnp.bfloat16)
        picked = picked + jnp.dot(chosen, kv_all[s], preferred_element_type=jnp.float32)
    cache_ref[...] = picked.astype(jnp.bfloat16).reshape(cache_ref.shape)

    for copy in sends:
        copy.wait_send()

    for step in range(4):
        kv_step(step, lambda copy: copy.wait_send())

    def drain(c, carry):
        for t in (3, 2):
            @pl.when((z > 0) & (z < t))
            def _():
                up_copy(c, t).wait_send()

            @pl.when((z < 3) & (z > 3 - t))
            def _():
                down_copy(c, 3 - t).wait_send()
        return carry

    lax.fori_loop(0, chunks, drain, 0)

    @pl.when(z == 0)
    def _():
        up_copy(chunks - 1, 2).wait_send()
        up_copy(chunks - 1, 1).wait_send()

    @pl.when(z == 3)
    def _():
        down_copy(chunks - 1, 1).wait_send()
        down_copy(chunks - 1, 2).wait_send()


def fused(hidden_in, norm_gain, query_proj, kv_proj, prompt_lengths, cache_slot):
    width = hidden_in.shape[1]
    query_cols = query_proj.shape[0]
    chunks = 1 + query_cols // BLK
    exponents = np.arange(HD // 2, dtype=np.float32) * 2.0 / HD
    frequency = np.float32(rope_base) ** -np.concatenate([exponents, exponents]).astype(np.float32)
    frequency = jnp.asarray(frequency[None, :])
    page_len = BLK // PAGES_DEV
    all_tokens = hidden_in.shape[0] * lax.axis_size("gx")
    window = all_tokens // 2 // BLK + 1
    bf16, f32 = jnp.bfloat16, jnp.float32
    dma = pltpu.SemaphoreType.DMA
    vmem = pl.BlockSpec(memory_space=pltpu.VMEM)
    return pl.pallas_call(
        fused_kernel,
        out_shape=(
            jax.ShapeDtypeStruct((BLK, query_cols), bf16),
            jax.ShapeDtypeStruct((PAGES_DEV, page_len, 2 * HD), bf16),
        ),
        in_specs=[vmem] * 7,
        out_specs=(vmem, vmem),
        scratch_shapes=[
            pltpu.VMEM((8, 8, 2 * BLK), f32),
            pltpu.VMEM((4, 8, 2 * BLK), f32),
            pltpu.VMEM((8, width), f32),
            pltpu.VMEM((8, width), f32),
            pltpu.VMEM((4, BLK, width), bf16),
            pltpu.VMEM((4, BLK, width), bf16),
            pltpu.VMEM((chunks, BLK, width), bf16),
            pltpu.VMEM((4, BLK, 2 * width), bf16),
            pltpu.VMEM((4, BLK, BLK), f32),
            pltpu.VMEM((chunks, BLK, BLK), f32),
            pltpu.VMEM((chunks, 4, BLK, BLK), bf16),
            pltpu.VMEM((chunks, 4, BLK, BLK), bf16),
            pltpu.VMEM((chunks, 4, BLK, BLK), bf16),
            pltpu.VMEM((chunks, 4, BLK, BLK), bf16),
            pltpu.VMEM((8, BLK, 2 * HD), bf16),
            pltpu.VMEM((BLK, window * BLK), f32),
            pltpu.VMEM((BLK, HD), f32),
            pltpu.VMEM((BLK, HD), f32),
            dma((8,)), dma((8,)), dma((4,)), dma((4,)), dma((2,)), dma((7,)), dma((4,)), dma((4,)),
            dma((chunks,)), dma((chunks,)), dma((chunks, 4)), dma((chunks, 4)), dma((chunks, 4)), dma((chunks, 4)),
            dma((2, 4)), dma((2, 4)), dma((8,)),
        ],
        compiler_params=pltpu.CompilerParams(
            collective_id=0, has_side_effects=True, vmem_limit_bytes=56 * 1024 * 1024
        ),
        cost_estimate=pl.CostEstimate(flops=4000000000, bytes_accessed=8000000, transcendentals=3000000),
    )(
        prompt_lengths[None, :], cache_slot[None, :], hidden_in, norm_gain[None, :], frequency, query_proj, kv_proj
    )


def solution(mesh):
    form = fused if (mesh.shape["gx"], mesh.shape["gy"]) == (4, 8) else local
    return jax.shard_map(
        form,
        mesh=mesh,
        in_specs=(P("gx", "gy"), P("gy"), P("gx", "gy"), P(None, "gy"), P(), P()),
        out_specs=(P("gy", "gx"), P("gy", None, "gx")),
        check_vma=False,
    )
```

```python
import math

import jax
import jax.numpy as jnp
import numpy as np
from jax import lax
from jax.experimental import pallas as pl
from jax.experimental.pallas import tpu as pltpu
from jax.sharding import PartitionSpec as P

MESH = pl.DeviceIdType.MESH

D = 4096
H = 32
KVH = 4
HD = 128
PAGES_DEV = 16


epsilon = 1e-06
rope_base = 5000000.0
masked_out = -1e30


def token_places(prompt_lengths, token_index):
    prompt_ends = jnp.cumsum(prompt_lengths)
    prompt_starts = prompt_ends - prompt_lengths
    segment = jnp.sum((token_index[:, None] >= prompt_ends[None, :]).astype(jnp.int32), axis=1)
    chosen = segment[:, None] == jnp.arange(prompt_lengths.shape[0], dtype=jnp.int32)[None, :]
    opening = jnp.sum(jnp.where(chosen, prompt_starts[None, :], 0), axis=1)
    return (segment, token_index - opening)


def rotate(vectors, places):
    half_size = vectors.shape[-1] // 2
    frequency = rope_base ** (-(jnp.arange(half_size, dtype=jnp.float32) * 2.0) / vectors.shape[-1])
    angles = places.astype(jnp.float32)[:, None] * frequency[None, :]
    cos_part = jnp.cos(angles)[:, None, :]
    sin_part = jnp.sin(angles)[:, None, :]
    leading = vectors[..., :half_size]
    trailing = vectors[..., half_size:]
    return jnp.concatenate(
        [leading * cos_part - trailing * sin_part, trailing * cos_part + leading * sin_part],
        axis=-1,
    )


def local(hidden_in, norm_gain, query_proj, kv_proj, prompt_lengths, cache_slot):
    count_gx = lax.axis_size("gx")
    count_gy = lax.axis_size("gy")
    where_gx = lax.axis_index("gx")
    where_gy = lax.axis_index("gy")
    local_rows = hidden_in.shape[0]
    block_tokens = local_rows * count_gx // count_gy
    all_tokens = block_tokens * count_gy
    heads_here = query_proj.shape[0] // HD
    group_size = H // KVH
    share = count_gx // KVH
    kv_head = where_gx * heads_here // group_size
    contract = (((1,), (1,)), ((), ()))
    kv_width = 2 * HD
    kv_start = kv_head * 2 * HD
    kv_rows = lax.dynamic_slice_in_dim(kv_proj, kv_start, kv_width, 0)
    widened = hidden_in.astype(jnp.float32)
    squares = jnp.sum(widened * widened, axis=1)
    totals = lax.psum(squares, "gy")
    normed = (
        widened * lax.rsqrt(totals / D + epsilon)[:, None] * norm_gain.astype(jnp.float32)[None, :]
    ).astype(jnp.bfloat16)
    gathered = lax.all_gather(normed, "gx", axis=0, tiled=True)
    stacked = jnp.concatenate([query_proj, kv_rows], axis=0)
    projected = lax.psum_scatter(
        lax.dot_general(gathered, stacked, contract, preferred_element_type=jnp.float32),
        "gy",
        scatter_dimension=0,
        tiled=True,
    )
    every_index = jnp.arange(all_tokens, dtype=jnp.int32)
    segment_all, place_all = token_places(prompt_lengths, every_index)
    first_query = where_gy * block_tokens
    token_index = first_query + jnp.arange(block_tokens, dtype=jnp.int32)
    segment_own = lax.dynamic_slice_in_dim(segment_all, first_query, block_tokens, 0)
    place_own = lax.dynamic_slice_in_dim(place_all, first_query, block_tokens, 0)
    query_cols = heads_here * HD
    queries = rotate(
        projected[:, :query_cols].reshape(block_tokens, heads_here, HD), place_own
    ).astype(jnp.bfloat16)
    keys = rotate(projected[:, query_cols : query_cols + HD][:, None, :], place_own)[
        :, 0, :
    ].astype(jnp.bfloat16)
    values = projected[:, query_cols + HD :].astype(jnp.bfloat16)
    if share == 2:
        cache_cols = jnp.where(where_gx % 2 == 0, keys, values)
    else:
        cache_cols = jnp.concatenate([keys, values], axis=1)
    score_scale = 1.0 / math.sqrt(HD)
    last_query = first_query + block_tokens - 1
    first_segment = segment_own[0]
    initial = (
        jnp.full((heads_here, block_tokens), masked_out, jnp.float32),
        jnp.zeros((heads_here, block_tokens), jnp.float32),
        jnp.zeros((heads_here, block_tokens, HD), jnp.float32),
    )
    key_piece = lax.all_gather(keys, "gy", axis=0, tiled=True)
    value_piece = lax.all_gather(values, "gy", axis=0, tiled=True)
    block_count = key_piece.shape[0] // block_tokens
    key_blocks = key_piece.reshape(block_count, block_tokens, HD)
    value_blocks = value_piece.reshape(block_count, block_tokens, HD)

    def one_block(current, inputs):
        key_rows, value_rows, offset = inputs
        block_begin = offset * block_tokens
        key_segment = lax.dynamic_slice_in_dim(segment_all, block_begin, block_tokens, 0)
        skipped = jnp.logical_or(
            block_begin > last_query, key_segment[block_tokens - 1] < first_segment
        )

        def compute(previous):
            running_max, running_sum, running_acc = previous
            key_index = block_begin + jnp.arange(block_tokens, dtype=jnp.int32)
            allowed = (key_segment[None, :] == segment_own[:, None]) & (
                key_index[None, :] <= token_index[:, None]
            )
            scores = (
                jnp.einsum("qhd,kd->hqk", queries, key_rows, preferred_element_type=jnp.float32)
                * score_scale
            )
            scores = jnp.where(allowed[None], scores, masked_out)
            new_max = jnp.maximum(running_max, jnp.max(scores, axis=2))
            weights = jnp.where(allowed[None], jnp.exp(scores - new_max[..., None]), 0.0)
            factor = jnp.exp(running_max - new_max)
            new_sum = running_sum * factor + jnp.sum(weights, axis=2)
            update = jnp.einsum(
                "hqk,kd->hqd",
                weights.astype(jnp.bfloat16),
                value_rows,
                preferred_element_type=jnp.float32,
            )
            return (new_max, new_sum, running_acc * factor[..., None] + update)

        return (lax.cond(skipped, lambda previous: previous, compute, current), None)

    offsets = jnp.arange(block_count, dtype=jnp.int32)
    result, unused = lax.scan(one_block, initial, (key_blocks, value_blocks, offsets))
    final_max, final_sum, final_acc = result
    attention = (
        (final_acc / final_sum[..., None])
        .transpose(1, 0, 2)
        .reshape(block_tokens, query_cols)
        .astype(jnp.bfloat16)
    )
    pages_dev = PAGES_DEV
    page_len = block_tokens // pages_dev
    width_cols = cache_cols.shape[1]
    my_pages = cache_cols.reshape(pages_dev, page_len * width_cols)
    capacity = max(1, pages_dev // count_gy)
    slots_all = count_gy * capacity
    owners = (cache_slot // pages_dev).reshape(count_gy, pages_dev)
    page_range = jnp.arange(pages_dev, dtype=jnp.int32)
    earlier = page_range[None, :] < page_range[:, None]
    same_owner = owners[:, :, None] == owners[:, None, :]
    ranks = jnp.sum((same_owner & earlier[None]).astype(jnp.int32), axis=2)
    my_owner = lax.dynamic_index_in_dim(owners, where_gy, 0, keepdims=False)
    my_rank = lax.dynamic_index_in_dim(ranks, where_gy, 0, keepdims=False)
    target = my_owner * capacity + my_rank
    slot_range = jnp.arange(slots_all, dtype=jnp.int32)
    send_map = (slot_range[:, None] == target[None, :]).astype(jnp.bfloat16)
    outgoing = jnp.dot(send_map, my_pages, preferred_element_type=jnp.float32).astype(jnp.bfloat16)
    outgoing = outgoing.reshape(count_gy, capacity * page_len * width_cols)
    incoming = lax.all_to_all(outgoing, "gy", split_axis=0, concat_axis=0, tiled=True)
    wanted = where_gy * pages_dev + page_range
    matches = cache_slot[None, :] == wanted[:, None]
    page_ids = jnp.arange(cache_slot.shape[0], dtype=jnp.int32)
    source_page = jnp.sum(jnp.where(matches, page_ids[None, :], 0), axis=1)
    source_rank = jnp.sum(jnp.where(matches, ranks.reshape(-1)[None, :], 0), axis=1)
    source_slot = source_page // pages_dev * capacity + source_rank
    take_map = (source_slot[:, None] == slot_range[None, :]).astype(jnp.bfloat16)
    cache_block = jnp.dot(
        take_map,
        incoming.reshape(slots_all, page_len * width_cols),
        preferred_element_type=jnp.float32,
    )
    cache_block = cache_block.astype(jnp.bfloat16).reshape(pages_dev, page_len, width_cols)
    return (attention, cache_block)


BLK = 256
TWO_PI_PARTS = (6.28125, 4059.0 / 2**21, 2.0 * math.pi - 6.28125 - 4059.0 / 2**21)


def fused_kernel(
    lengths_ref, slot_ref, hid_ref, gain_row, freq_ref, wq_ref, wkv_ref,
    out_ref, cache_ref,
    squares, inverse, gain_ref, gain_other, x_own, x_other, w_other, normed, part, final,
    up_out, up_in, down_out, down_in, kv_all, bias, cos_ref, sin_ref,
    sq_send, sq_recv, inv_send, inv_recv, gain_sem, x_send, xo_recv, xn_recv,
    w_send, w_recv, up_send, up_recv, down_send, down_recv, kz_send, ky_send, kv_recv,
):
    gx = lax.axis_index("gx")
    gy = lax.axis_index("gy")
    y = lax.rem(gy, 2)
    z = lax.div(gy, 2)
    core_peer = gx + 1 - 2 * lax.rem(gx, 2)
    x_peer = lax.rem(gx + 2, 4)
    far_peer = 3 - gx
    y_peer = gy + 1 - 2 * y
    depth = hid_ref.shape[1]
    chunks = w_other.shape[0]

    def remote(src, dst, send_sem, recv_sem, to_gx, to_gy):
        return pltpu.make_async_remote_copy(
            src_ref=src, dst_ref=dst, send_sem=send_sem, recv_sem=recv_sem,
            device_id=(to_gx, to_gy), device_id_type=MESH,
        )

    barrier = pltpu.get_barrier_semaphore()
    for step in range(1, 8):
        pl.semaphore_signal(barrier, inc=1, device_id=(gx, lax.rem(gy + step, 8)), device_id_type=MESH)
    for step in range(1, 4):
        pl.semaphore_signal(barrier, inc=1, device_id=(lax.rem(gx + step, 4), gy), device_id_type=MESH)

    widened = hid_ref[...].astype(jnp.float32)
    squares[gy] = lax.dot_general(
        jnp.ones((8, depth), jnp.float32), widened * widened, (((1,), (1,)), ((), ())),
        precision=lax.Precision.HIGHEST, preferred_element_type=jnp.float32,
    )
    own_rows = pl.ds(pl.multiple_of(y * BLK, BLK), BLK)
    other_rows = pl.ds(pl.multiple_of((1 - y) * BLK, BLK), BLK)
    x_own[gx] = hid_ref[own_rows, :]
    gain_ref[...] = jnp.broadcast_to(gain_row[...].astype(jnp.float32), gain_ref.shape)
    pl.semaphore_wait(barrier, 10)

    sends = []

    def go(copy):
        copy.start()
        sends.append(copy)

    for step in range(1, 8):
        go(remote(squares.at[gy], squares.at[gy], sq_send.at[step], sq_recv.at[gy], gx, lax.rem(gy + step, 8)))
    go(remote(gain_ref, gain_other, gain_sem.at[0], gain_sem.at[1], gx, y_peer))
    go(remote(hid_ref.at[other_rows, :], x_other.at[gx], x_send.at[0], xn_recv.at[gx], gx, y_peer))
    go(remote(hid_ref.at[own_rows, :], x_own.at[gx], x_send.at[1], xo_recv.at[gx], x_peer, gy))
    go(remote(hid_ref.at[own_rows, :], x_own.at[gx], x_send.at[2], xo_recv.at[gx], core_peer, gy))
    kv_rows = pl.ds(pl.multiple_of(gx * 2 * HD, 2 * HD), 2 * HD)

    def send_weights(c):
        rows = wkv_ref.at[kv_rows, :] if c == 0 else wq_ref.at[pl.ds((c - 1) * BLK, BLK), :]
        go(remote(rows, w_other.at[c], w_send.at[c], w_recv.at[c], gx, y_peer))

    def arrived(dst, recv_sem):
        remote(dst, dst, x_send.at[0], recv_sem, gx, y_peer).wait_recv()

    first_token = gy * BLK
    token = first_token + lax.broadcasted_iota(jnp.int32, (BLK, HD), 0)
    opening = jnp.zeros((BLK, HD), jnp.int32)
    end = jnp.zeros((1, HD), jnp.int32)
    for s in range(lengths_ref.shape[1]):
        end = end + lengths_ref[0:1, s : s + 1]
        opening = jnp.where(token >= end, end, opening)
    angles = (token - opening).astype(jnp.float32) * freq_ref[0:1, :]
    turns = jnp.floor(angles * (0.5 / math.pi) + 0.5)
    for piece in TWO_PI_PARTS:
        angles = angles - turns * piece
    cos_ref[...] = jnp.cos(angles)
    sign = jnp.where(lax.broadcasted_iota(jnp.int32, (BLK, HD), 1) < HD // 2, -1.0, 1.0)
    sin_ref[...] = jnp.sin(angles) * sign
    window = bias.shape[1] // BLK
    start_block = jnp.maximum(gy - (window - 1), 0)
    for s in range(window):
        for half in range(2):
            lanes = s * BLK + half * HD
            key = start_block * BLK + lanes + lax.broadcasted_iota(jnp.int32, (BLK, HD), 1)
            bias[:, lanes : lanes + HD] = jnp.where((key >= opening) & (key <= token), 0.0, masked_out)

    for step in range(1, 8):
        source = lax.rem(gy + step, 8)
        arrived(squares.at[source], sq_recv.at[source])
    total = squares[0]
    for s in range(1, 8):
        total = total + squares[s]
    inverse[gx] = lax.rsqrt(total / D + epsilon)
    for step in range(1, 4):
        go(remote(inverse.at[gx], inverse.at[gx], inv_send.at[step], inv_recv.at[gx], lax.rem(gx + step, 4), gy))

    eighth = jnp.full((8, depth), 0.125, jnp.float32)

    def normalise(m):
        scale = lax.dot_general(
            inverse[m, :, own_rows], eighth, (((0,), (0,)), ((), ())),
            precision=lax.Precision.HIGHEST, preferred_element_type=jnp.float32,
        )
        normed[m, :, 0:depth] = (x_own[m].astype(jnp.float32) * scale * gain_ref[0:1, :]).astype(jnp.bfloat16)
        normed[m, :, depth:] = (x_other[m].astype(jnp.float32) * scale * gain_other[0:1, :]).astype(jnp.bfloat16)

    arrived(x_other.at[gx], xn_recv.at[gx])
    go(remote(x_other.at[gx], x_other.at[gx], x_send.at[3], xn_recv.at[gx], x_peer, gy))
    go(remote(x_other.at[gx], x_other.at[gx], x_send.at[4], xn_recv.at[gx], core_peer, gy))
    send_weights(0)
    arrived(x_own.at[x_peer], xo_recv.at[x_peer])
    go(remote(x_own.at[x_peer], x_own.at[x_peer], x_send.at[5], xo_recv.at[x_peer], core_peer, gy))
    arrived(gain_other, gain_sem.at[1])
    normalise(gx)
    arrived(x_own.at[core_peer], xo_recv.at[core_peer])
    arrived(x_other.at[core_peer], xn_recv.at[core_peer])
    arrived(inverse.at[core_peer], inv_recv.at[core_peer])
    normalise(core_peer)
    arrived(x_other.at[x_peer], xn_recv.at[x_peer])
    go(remote(x_other.at[x_peer], x_other.at[x_peer], x_send.at[6], xn_recv.at[x_peer], core_peer, gy))
    send_weights(1)
    arrived(inverse.at[x_peer], inv_recv.at[x_peer])
    normalise(x_peer)
    arrived(inverse.at[far_peer], inv_recv.at[far_peer])
    arrived(x_own.at[far_peer], xo_recv.at[far_peer])
    arrived(x_other.at[far_peer], xn_recv.at[far_peer])
    normalise(far_peer)

    contract = (((1,), (1,)), ((), ()))

    def multiply(c, w_here):
        arrived(w_other.at[c], w_recv.at[c])
        if isinstance(c, int) and c + 2 < chunks:
            send_weights(c + 2)

        def one(m, carry):
            part[m] = lax.dot_general(
                normed[m, :, 0:depth], w_here(), contract, preferred_element_type=jnp.float32
            ) + lax.dot_general(
                normed[m, :, depth:], w_other[c], contract, preferred_element_type=jnp.float32
            )
            return carry

        lax.fori_loop(0, 4, one, 0)
        final[c] = part[z]

    def start_of_chain(c):
        return isinstance(c, int) and c == 0

    def up_copy(c, t):
        return remote(up_out.at[c, t], up_in.at[c, t], up_send.at[c, t], up_recv.at[c, t], gx, gy + 2)

    def down_copy(c, t):
        return remote(down_out.at[c, t], down_in.at[c, t], down_send.at[c, t], down_recv.at[c, t], gx, gy - 2)

    def pass_on(c, beside=None):
        for t in (3, 2, 1):
            @pl.when(z == 0)
            def _():
                if t == 1:
                    up_copy(c, 3).wait_send()
                elif not start_of_chain(c):
                    up_copy(c - 1, t - 1).wait_send()
                up_out[c, t] = part[t].astype(jnp.bfloat16)
                up_copy(c, t).start()

            @pl.when((z > 0) & (z < t))
            def _():
                arrived(up_in.at[c, t], up_recv.at[c, t])
                up_out[c, t] = (part[t] + up_in[c, t].astype(jnp.float32)).astype(jnp.bfloat16)
                up_copy(c, t).start()

            d = 3 - t

            @pl.when(z == 3)
            def _():
                if t == 1:
                    down_copy(c, 0).wait_send()
                elif not start_of_chain(c):
                    down_copy(c - 1, d + 1).wait_send()
                down_out[c, d] = part[d].astype(jnp.bfloat16)
                down_copy(c, d).start()

            @pl.when((z < 3) & (z > d))
            def _():
                arrived(down_in.at[c, d], down_recv.at[c, d])
                down_out[c, d] = (part[d] + down_in[c, d].astype(jnp.float32)).astype(jnp.bfloat16)
                down_copy(c, d).start()

            if beside is not None:
                beside(3 - t)

    def finish(c):
        @pl.when(z > 0)
        def _():
            arrived(up_in.at[c, z], up_recv.at[c, z])
            final[c] = final[c] + up_in[c, z].astype(jnp.float32)

        @pl.when(z < 3)
        def _():
            arrived(down_in.at[c, z], down_recv.at[c, z])
            final[c] = final[c] + down_in[c, z].astype(jnp.float32)

    def rotated(u):
        return (u * cos_ref[...] + pltpu.roll(u, HD // 2, 1) * sin_ref[...]).astype(jnp.bfloat16)

    def q_chunk(c, beside):
        rows = pl.ds(pl.multiple_of((c - 1) * BLK, BLK), BLK)
        multiply(c, lambda: wq_ref[rows, :])
        pass_on(c, beside)

    def kv_up(step):
        block = kv_all.at[gy - 2 * step]
        return remote(block, block, kz_send.at[0, step], kv_recv.at[gy - 2 * step], gx, gy + 2)

    def kv_down(step):
        block = kv_all.at[gy + 2 * step]
        return remote(block, block, kz_send.at[1, step], kv_recv.at[gy + 2 * step], gx, gy - 2)

    def kv_across(source, side, step):
        return remote(kv_all.at[source], kv_all.at[source], ky_send.at[side, step], kv_recv.at[source], gx, y_peer)

    def kv_step(step, act):
        @pl.when((z >= step) & (z < 3))
        def _():
            act(kv_up(step))

        @pl.when((z + step <= 3) & (z > 0))
        def _():
            act(kv_down(step))

        if step == 0:
            act(kv_across(gy, 0, 0))
        else:
            @pl.when(z >= step)
            def _():
                act(kv_across(gy - 2 * step, 0, step))

            @pl.when(z + step <= 3)
            def _():
                act(kv_across(gy + 2 * step, 1, step))

    def kv_forward(step):
        @pl.when(z >= step)
        def _():
            arrived(kv_all.at[gy - 2 * step], kv_recv.at[gy - 2 * step])

        @pl.when(z + step <= 3)
        def _():
            arrived(kv_all.at[gy + 2 * step], kv_recv.at[gy + 2 * step])

        kv_step(step, lambda copy: copy.start())

    score_scale = math.log2(math.e) / math.sqrt(HD)
    keys = pl.ds(start_block, window)

    def attend(head):
        c = 1 + lax.div(head, 2)

        @pl.when(lax.rem(head, 2) == 0)
        def _():
            finish(c)

        lanes = pl.ds(pl.multiple_of(lax.rem(head, 2) * HD, HD), HD)
        query = rotated(final[c, :, lanes])
        key_rows = kv_all[keys, :, 0:HD].reshape(window * BLK, HD)
        value_rows = kv_all[keys, :, HD:].reshape(window * BLK, HD)
        scores = lax.dot_general(query, key_rows, contract, preferred_element_type=jnp.float32)
        scores = scores * score_scale + bias[...]
        weights = jnp.exp2(scores - jnp.max(scores, axis=1, keepdims=True))
        sums = jnp.sum(weights, axis=1, keepdims=True)
        mixed = jnp.dot(weights.astype(jnp.bfloat16), value_rows, preferred_element_type=jnp.float32)
        out_ref[:, pl.ds(pl.multiple_of(head * HD, HD), HD)] = (mixed / sums).astype(jnp.bfloat16)

    def share_kv(step):
        if step == 1:
            finish(0)
            kv_all[gy, :, 0:HD] = rotated(final[0, :, 0:HD])
            kv_all[gy, :, HD:] = final[0, :, HD:].astype(jnp.bfloat16)
            kv_step(0, lambda copy: copy.start())

    multiply(0, lambda: wkv_ref[kv_rows, :])
    pass_on(0)
    q_chunk(1, share_kv)
    q_chunk(2, lambda step: kv_forward(step + 1))
    for step in range(4):
        source = lax.rem(y_peer + 2 * step, 8)
        arrived(kv_all.at[source], kv_recv.at[source])

    early = 3 * (chunks - 3)

    def late_chunk(c, carry):
        q_chunk(c, lambda step: attend((c - 3) * 3 + step))
        return carry

    lax.fori_loop(3, chunks, late_chunk, 0)

    page_len = cache_ref.shape[1]
    pages = slot_ref.shape[1]
    wanted = (gy * BLK + lax.broadcasted_iota(jnp.int32, (BLK, BLK), 0)).astype(jnp.float32)
    page = lax.broadcasted_iota(jnp.int32, (pages, BLK), 0)
    lane = lax.broadcasted_iota(jnp.int32, (pages, BLK), 1)
    offset = lax.rem(lane[0:8, :], page_len).astype(jnp.float32)
    slots = jnp.broadcast_to(slot_ref[...].astype(jnp.float32), (8, pages)).astype(jnp.bfloat16)
    picked = jnp.zeros((BLK, 2 * HD), jnp.float32)
    for s in range(8):
        spread = jnp.where(page == s * PAGES_DEV + lax.div(lane, page_len), 1.0, 0.0).astype(jnp.bfloat16)
        places = jnp.dot(slots, spread, preferred_element_type=jnp.float32) * page_len + offset
        chosen = jnp.where(places[0:1, :] == wanted, 1.0, 0.0).astype(jnp.bfloat16)
        picked = picked + jnp.dot(chosen, kv_all[s], preferred_element_type=jnp.float32)
    cache_ref[...] = picked.astype(jnp.bfloat16).reshape(cache_ref.shape)

    def late_head(head, carry):
        attend(head)
        return carry

    lax.fori_loop(early, 2 * (chunks - 1), late_head, 0)

    for copy in sends:
        copy.wait_send()

    for step in range(4):
        kv_step(step, lambda copy: copy.wait_send())

    def drain(c, carry):
        for t in (3, 2):
            @pl.when((z > 0) & (z < t))
            def _():
                up_copy(c, t).wait_send()

            @pl.when((z < 3) & (z > 3 - t))
            def _():
                down_copy(c, 3 - t).wait_send()
        return carry

    lax.fori_loop(0, chunks, drain, 0)

    @pl.when(z == 0)
    def _():
        up_copy(chunks - 1, 2).wait_send()
        up_copy(chunks - 1, 1).wait_send()

    @pl.when(z == 3)
    def _():
        down_copy(chunks - 1, 1).wait_send()
        down_copy(chunks - 1, 2).wait_send()


def fused(hidden_in, norm_gain, query_proj, kv_proj, prompt_lengths, cache_slot):
    width = hidden_in.shape[1]
    query_cols = query_proj.shape[0]
    chunks = 1 + query_cols // BLK
    exponents = np.arange(HD // 2, dtype=np.float32) * 2.0 / HD
    frequency = np.float32(rope_base) ** -np.concatenate([exponents, exponents]).astype(np.float32)
    frequency = jnp.asarray(frequency[None, :])
    page_len = BLK // PAGES_DEV
    all_tokens = hidden_in.shape[0] * lax.axis_size("gx")
    window = all_tokens // 2 // BLK + 1
    bf16, f32 = jnp.bfloat16, jnp.float32
    dma = pltpu.SemaphoreType.DMA
    vmem = pl.BlockSpec(memory_space=pltpu.VMEM)
    return pl.pallas_call(
        fused_kernel,
        out_shape=(
            jax.ShapeDtypeStruct((BLK, query_cols), bf16),
            jax.ShapeDtypeStruct((PAGES_DEV, page_len, 2 * HD), bf16),
        ),
        in_specs=[vmem] * 7,
        out_specs=(vmem, vmem),
        scratch_shapes=[
            pltpu.VMEM((8, 8, 2 * BLK), f32),
            pltpu.VMEM((4, 8, 2 * BLK), f32),
            pltpu.VMEM((8, width), f32),
            pltpu.VMEM((8, width), f32),
            pltpu.VMEM((4, BLK, width), bf16),
            pltpu.VMEM((4, BLK, width), bf16),
            pltpu.VMEM((chunks, BLK, width), bf16),
            pltpu.VMEM((4, BLK, 2 * width), bf16),
            pltpu.VMEM((4, BLK, BLK), f32),
            pltpu.VMEM((chunks, BLK, BLK), f32),
            pltpu.VMEM((chunks, 4, BLK, BLK), bf16),
            pltpu.VMEM((chunks, 4, BLK, BLK), bf16),
            pltpu.VMEM((chunks, 4, BLK, BLK), bf16),
            pltpu.VMEM((chunks, 4, BLK, BLK), bf16),
            pltpu.VMEM((8, BLK, 2 * HD), bf16),
            pltpu.VMEM((BLK, window * BLK), f32),
            pltpu.VMEM((BLK, HD), f32),
            pltpu.VMEM((BLK, HD), f32),
            dma((8,)), dma((8,)), dma((4,)), dma((4,)), dma((2,)), dma((7,)), dma((4,)), dma((4,)),
            dma((chunks,)), dma((chunks,)), dma((chunks, 4)), dma((chunks, 4)), dma((chunks, 4)), dma((chunks, 4)),
            dma((2, 4)), dma((2, 4)), dma((8,)),
        ],
        compiler_params=pltpu.CompilerParams(
            collective_id=0, has_side_effects=True, vmem_limit_bytes=56 * 1024 * 1024
        ),
        cost_estimate=pl.CostEstimate(flops=4000000000, bytes_accessed=8000000, transcendentals=3000000),
    )(
        prompt_lengths[None, :], cache_slot[None, :], hidden_in, norm_gain[None, :], frequency, query_proj, kv_proj
    )


def solution(mesh):
    form = fused if (mesh.shape["gx"], mesh.shape["gy"]) == (4, 8) else local
    return jax.shard_map(
        form,
        mesh=mesh,
        in_specs=(P("gx", "gy"), P("gy"), P("gx", "gy"), P(None, "gy"), P(), P()),
        out_specs=(P("gy", "gx"), P("gy", None, "gx")),
        check_vma=False,
    )
```

```python
import math

import jax
import jax.numpy as jnp
import numpy as np
from jax import lax
from jax.experimental import pallas as pl
from jax.experimental.pallas import tpu as pltpu
from jax.sharding import PartitionSpec as P

MESH = pl.DeviceIdType.MESH

D = 4096
H = 32
KVH = 4
HD = 128
PAGES_DEV = 16


epsilon = 1e-06
rope_base = 5000000.0
masked_out = -1e30


def token_places(prompt_lengths, token_index):
    prompt_ends = jnp.cumsum(prompt_lengths)
    prompt_starts = prompt_ends - prompt_lengths
    segment = jnp.sum((token_index[:, None] >= prompt_ends[None, :]).astype(jnp.int32), axis=1)
    chosen = segment[:, None] == jnp.arange(prompt_lengths.shape[0], dtype=jnp.int32)[None, :]
    opening = jnp.sum(jnp.where(chosen, prompt_starts[None, :], 0), axis=1)
    return (segment, token_index - opening)


def rotate(vectors, places):
    half_size = vectors.shape[-1] // 2
    frequency = rope_base ** (-(jnp.arange(half_size, dtype=jnp.float32) * 2.0) / vectors.shape[-1])
    angles = places.astype(jnp.float32)[:, None] * frequency[None, :]
    cos_part = jnp.cos(angles)[:, None, :]
    sin_part = jnp.sin(angles)[:, None, :]
    leading = vectors[..., :half_size]
    trailing = vectors[..., half_size:]
    return jnp.concatenate(
        [leading * cos_part - trailing * sin_part, trailing * cos_part + leading * sin_part],
        axis=-1,
    )


def local(hidden_in, norm_gain, query_proj, kv_proj, prompt_lengths, cache_slot):
    count_gx = lax.axis_size("gx")
    count_gy = lax.axis_size("gy")
    where_gx = lax.axis_index("gx")
    where_gy = lax.axis_index("gy")
    local_rows = hidden_in.shape[0]
    block_tokens = local_rows * count_gx // count_gy
    all_tokens = block_tokens * count_gy
    heads_here = query_proj.shape[0] // HD
    group_size = H // KVH
    share = count_gx // KVH
    kv_head = where_gx * heads_here // group_size
    contract = (((1,), (1,)), ((), ()))
    kv_width = 2 * HD
    kv_start = kv_head * 2 * HD
    kv_rows = lax.dynamic_slice_in_dim(kv_proj, kv_start, kv_width, 0)
    widened = hidden_in.astype(jnp.float32)
    squares = jnp.sum(widened * widened, axis=1)
    totals = lax.psum(squares, "gy")
    normed = (
        widened * lax.rsqrt(totals / D + epsilon)[:, None] * norm_gain.astype(jnp.float32)[None, :]
    ).astype(jnp.bfloat16)
    gathered = lax.all_gather(normed, "gx", axis=0, tiled=True)
    stacked = jnp.concatenate([query_proj, kv_rows], axis=0)
    projected = lax.psum_scatter(
        lax.dot_general(gathered, stacked, contract, preferred_element_type=jnp.float32),
        "gy",
        scatter_dimension=0,
        tiled=True,
    )
    every_index = jnp.arange(all_tokens, dtype=jnp.int32)
    segment_all, place_all = token_places(prompt_lengths, every_index)
    first_query = where_gy * block_tokens
    token_index = first_query + jnp.arange(block_tokens, dtype=jnp.int32)
    segment_own = lax.dynamic_slice_in_dim(segment_all, first_query, block_tokens, 0)
    place_own = lax.dynamic_slice_in_dim(place_all, first_query, block_tokens, 0)
    query_cols = heads_here * HD
    queries = rotate(
        projected[:, :query_cols].reshape(block_tokens, heads_here, HD), place_own
    ).astype(jnp.bfloat16)
    keys = rotate(projected[:, query_cols : query_cols + HD][:, None, :], place_own)[
        :, 0, :
    ].astype(jnp.bfloat16)
    values = projected[:, query_cols + HD :].astype(jnp.bfloat16)
    if share == 2:
        cache_cols = jnp.where(where_gx % 2 == 0, keys, values)
    else:
        cache_cols = jnp.concatenate([keys, values], axis=1)
    score_scale = 1.0 / math.sqrt(HD)
    last_query = first_query + block_tokens - 1
    first_segment = segment_own[0]
    initial = (
        jnp.full((heads_here, block_tokens), masked_out, jnp.float32),
        jnp.zeros((heads_here, block_tokens), jnp.float32),
        jnp.zeros((heads_here, block_tokens, HD), jnp.float32),
    )
    key_piece = lax.all_gather(keys, "gy", axis=0, tiled=True)
    value_piece = lax.all_gather(values, "gy", axis=0, tiled=True)
    block_count = key_piece.shape[0] // block_tokens
    key_blocks = key_piece.reshape(block_count, block_tokens, HD)
    value_blocks = value_piece.reshape(block_count, block_tokens, HD)

    def one_block(current, inputs):
        key_rows, value_rows, offset = inputs
        block_begin = offset * block_tokens
        key_segment = lax.dynamic_slice_in_dim(segment_all, block_begin, block_tokens, 0)
        skipped = jnp.logical_or(
            block_begin > last_query, key_segment[block_tokens - 1] < first_segment
        )

        def compute(previous):
            running_max, running_sum, running_acc = previous
            key_index = block_begin + jnp.arange(block_tokens, dtype=jnp.int32)
            allowed = (key_segment[None, :] == segment_own[:, None]) & (
                key_index[None, :] <= token_index[:, None]
            )
            scores = (
                jnp.einsum("qhd,kd->hqk", queries, key_rows, preferred_element_type=jnp.float32)
                * score_scale
            )
            scores = jnp.where(allowed[None], scores, masked_out)
            new_max = jnp.maximum(running_max, jnp.max(scores, axis=2))
            weights = jnp.where(allowed[None], jnp.exp(scores - new_max[..., None]), 0.0)
            factor = jnp.exp(running_max - new_max)
            new_sum = running_sum * factor + jnp.sum(weights, axis=2)
            update = jnp.einsum(
                "hqk,kd->hqd",
                weights.astype(jnp.bfloat16),
                value_rows,
                preferred_element_type=jnp.float32,
            )
            return (new_max, new_sum, running_acc * factor[..., None] + update)

        return (lax.cond(skipped, lambda previous: previous, compute, current), None)

    offsets = jnp.arange(block_count, dtype=jnp.int32)
    result, unused = lax.scan(one_block, initial, (key_blocks, value_blocks, offsets))
    final_max, final_sum, final_acc = result
    attention = (
        (final_acc / final_sum[..., None])
        .transpose(1, 0, 2)
        .reshape(block_tokens, query_cols)
        .astype(jnp.bfloat16)
    )
    pages_dev = PAGES_DEV
    page_len = block_tokens // pages_dev
    width_cols = cache_cols.shape[1]
    my_pages = cache_cols.reshape(pages_dev, page_len * width_cols)
    capacity = max(1, pages_dev // count_gy)
    slots_all = count_gy * capacity
    owners = (cache_slot // pages_dev).reshape(count_gy, pages_dev)
    page_range = jnp.arange(pages_dev, dtype=jnp.int32)
    earlier = page_range[None, :] < page_range[:, None]
    same_owner = owners[:, :, None] == owners[:, None, :]
    ranks = jnp.sum((same_owner & earlier[None]).astype(jnp.int32), axis=2)
    my_owner = lax.dynamic_index_in_dim(owners, where_gy, 0, keepdims=False)
    my_rank = lax.dynamic_index_in_dim(ranks, where_gy, 0, keepdims=False)
    target = my_owner * capacity + my_rank
    slot_range = jnp.arange(slots_all, dtype=jnp.int32)
    send_map = (slot_range[:, None] == target[None, :]).astype(jnp.bfloat16)
    outgoing = jnp.dot(send_map, my_pages, preferred_element_type=jnp.float32).astype(jnp.bfloat16)
    outgoing = outgoing.reshape(count_gy, capacity * page_len * width_cols)
    incoming = lax.all_to_all(outgoing, "gy", split_axis=0, concat_axis=0, tiled=True)
    wanted = where_gy * pages_dev + page_range
    matches = cache_slot[None, :] == wanted[:, None]
    page_ids = jnp.arange(cache_slot.shape[0], dtype=jnp.int32)
    source_page = jnp.sum(jnp.where(matches, page_ids[None, :], 0), axis=1)
    source_rank = jnp.sum(jnp.where(matches, ranks.reshape(-1)[None, :], 0), axis=1)
    source_slot = source_page // pages_dev * capacity + source_rank
    take_map = (source_slot[:, None] == slot_range[None, :]).astype(jnp.bfloat16)
    cache_block = jnp.dot(
        take_map,
        incoming.reshape(slots_all, page_len * width_cols),
        preferred_element_type=jnp.float32,
    )
    cache_block = cache_block.astype(jnp.bfloat16).reshape(pages_dev, page_len, width_cols)
    return (attention, cache_block)


BLK = 256
TWO_PI_PARTS = (6.28125, 4059.0 / 2**21, 2.0 * math.pi - 6.28125 - 4059.0 / 2**21)


def fused_kernel(
    lengths_ref, slot_ref, hid_ref, gain_row, freq_ref, wq_ref, wkv_ref,
    out_ref, cache_ref,
    squares, inverse, gain_ref, gain_other, x_own, x_other, w_other, normed, part, final,
    up_out, up_in, down_out, down_in, kv_all, bias, cos_ref, sin_ref,
    sq_send, sq_recv, inv_send, inv_recv, gain_sem, x_send, xo_recv, xn_recv,
    w_send, w_recv, up_send, up_recv, down_send, down_recv, kz_send, ky_send, kv_recv,
):
    gx = lax.axis_index("gx")
    gy = lax.axis_index("gy")
    y = lax.rem(gy, 2)
    z = lax.div(gy, 2)
    core_peer = gx + 1 - 2 * lax.rem(gx, 2)
    x_peer = lax.rem(gx + 2, 4)
    far_peer = 3 - gx
    y_peer = gy + 1 - 2 * y
    depth = hid_ref.shape[1]
    chunks = w_other.shape[0]

    def remote(src, dst, send_sem, recv_sem, to_gx, to_gy):
        return pltpu.make_async_remote_copy(
            src_ref=src, dst_ref=dst, send_sem=send_sem, recv_sem=recv_sem,
            device_id=(to_gx, to_gy), device_id_type=MESH,
        )

    barrier = pltpu.get_barrier_semaphore()
    for step in range(1, 8):
        pl.semaphore_signal(barrier, inc=1, device_id=(gx, lax.rem(gy + step, 8)), device_id_type=MESH)
    for step in range(1, 4):
        pl.semaphore_signal(barrier, inc=1, device_id=(lax.rem(gx + step, 4), gy), device_id_type=MESH)

    widened = hid_ref[...].astype(jnp.float32)
    squares[gy] = lax.dot_general(
        jnp.ones((8, depth), jnp.float32), widened * widened, (((1,), (1,)), ((), ())),
        precision=lax.Precision.HIGHEST, preferred_element_type=jnp.float32,
    )
    own_rows = pl.ds(pl.multiple_of(y * BLK, BLK), BLK)
    other_rows = pl.ds(pl.multiple_of((1 - y) * BLK, BLK), BLK)
    x_own[gx] = hid_ref[own_rows, :]
    gain_ref[...] = jnp.broadcast_to(gain_row[...].astype(jnp.float32), gain_ref.shape)
    pl.semaphore_wait(barrier, 10)

    sends = []

    def go(copy):
        copy.start()
        sends.append(copy)

    for step in range(1, 8):
        go(remote(squares.at[gy], squares.at[gy], sq_send.at[step], sq_recv.at[gy], gx, lax.rem(gy + step, 8)))
    go(remote(gain_ref, gain_other, gain_sem.at[0], gain_sem.at[1], gx, y_peer))
    go(remote(hid_ref.at[other_rows, :], x_other.at[gx], x_send.at[0], xn_recv.at[gx], gx, y_peer))
    go(remote(hid_ref.at[own_rows, :], x_own.at[gx], x_send.at[1], xo_recv.at[gx], x_peer, gy))
    go(remote(hid_ref.at[own_rows, :], x_own.at[gx], x_send.at[2], xo_recv.at[gx], core_peer, gy))
    kv_rows = pl.ds(pl.multiple_of(gx * 2 * HD, 2 * HD), 2 * HD)

    def send_weights(c):
        rows = wkv_ref.at[kv_rows, :] if c == 0 else wq_ref.at[pl.ds((c - 1) * BLK, BLK), :]
        go(remote(rows, w_other.at[c], w_send.at[c], w_recv.at[c], gx, y_peer))

    def arrived(dst, recv_sem):
        remote(dst, dst, x_send.at[0], recv_sem, gx, y_peer).wait_recv()

    first_token = gy * BLK
    token = first_token + lax.broadcasted_iota(jnp.int32, (BLK, HD), 0)
    opening = jnp.zeros((BLK, HD), jnp.int32)
    end = jnp.zeros((1, HD), jnp.int32)
    for s in range(lengths_ref.shape[1]):
        end = end + lengths_ref[0:1, s : s + 1]
        opening = jnp.where(token >= end, end, opening)
    angles = (token - opening).astype(jnp.float32) * freq_ref[0:1, :]
    turns = jnp.floor(angles * (0.5 / math.pi) + 0.5)
    for piece in TWO_PI_PARTS:
        angles = angles - turns * piece
    cos_ref[...] = jnp.cos(angles)
    sign = jnp.where(lax.broadcasted_iota(jnp.int32, (BLK, HD), 1) < HD // 2, -1.0, 1.0)
    sin_ref[...] = jnp.sin(angles) * sign
    window = bias.shape[1] // BLK
    start_block = jnp.maximum(gy - (window - 1), 0)
    for s in range(window):
        for half in range(2):
            lanes = s * BLK + half * HD
            key = start_block * BLK + lanes + lax.broadcasted_iota(jnp.int32, (BLK, HD), 1)
            bias[:, lanes : lanes + HD] = jnp.where((key >= opening) & (key <= token), 0.0, masked_out)

    for step in range(1, 8):
        source = lax.rem(gy + step, 8)
        arrived(squares.at[source], sq_recv.at[source])
    total = squares[0]
    for s in range(1, 8):
        total = total + squares[s]
    inverse[gx] = lax.rsqrt(total / D + epsilon)
    for step in range(1, 4):
        go(remote(inverse.at[gx], inverse.at[gx], inv_send.at[step], inv_recv.at[gx], lax.rem(gx + step, 4), gy))

    eighth = jnp.full((8, depth), 0.125, jnp.float32)

    def normalise(m):
        scale = lax.dot_general(
            inverse[m, :, own_rows], eighth, (((0,), (0,)), ((), ())),
            precision=lax.Precision.HIGHEST, preferred_element_type=jnp.float32,
        )
        normed[m, :, 0:depth] = (x_own[m].astype(jnp.float32) * scale * gain_ref[0:1, :]).astype(jnp.bfloat16)
        normed[m, :, depth:] = (x_other[m].astype(jnp.float32) * scale * gain_other[0:1, :]).astype(jnp.bfloat16)

    arrived(x_other.at[gx], xn_recv.at[gx])
    go(remote(x_other.at[gx], x_other.at[gx], x_send.at[3], xn_recv.at[gx], x_peer, gy))
    go(remote(x_other.at[gx], x_other.at[gx], x_send.at[4], xn_recv.at[gx], core_peer, gy))
    send_weights(0)
    arrived(x_own.at[x_peer], xo_recv.at[x_peer])
    go(remote(x_own.at[x_peer], x_own.at[x_peer], x_send.at[5], xo_recv.at[x_peer], core_peer, gy))
    arrived(gain_other, gain_sem.at[1])
    normalise(gx)
    arrived(x_own.at[core_peer], xo_recv.at[core_peer])
    arrived(x_other.at[core_peer], xn_recv.at[core_peer])
    arrived(inverse.at[core_peer], inv_recv.at[core_peer])
    normalise(core_peer)
    arrived(x_other.at[x_peer], xn_recv.at[x_peer])
    go(remote(x_other.at[x_peer], x_other.at[x_peer], x_send.at[6], xn_recv.at[x_peer], core_peer, gy))
    send_weights(1)
    arrived(inverse.at[x_peer], inv_recv.at[x_peer])
    normalise(x_peer)
    arrived(inverse.at[far_peer], inv_recv.at[far_peer])
    arrived(x_own.at[far_peer], xo_recv.at[far_peer])
    arrived(x_other.at[far_peer], xn_recv.at[far_peer])
    normalise(far_peer)

    contract = (((1,), (1,)), ((), ()))

    def multiply(c, w_here):
        arrived(w_other.at[c], w_recv.at[c])
        if isinstance(c, int) and c + 2 < chunks:
            send_weights(c + 2)

        def one(m, carry):
            part[c % 2, m] = lax.dot_general(
                normed[m, :, 0:depth], w_here(), contract, preferred_element_type=jnp.float32
            ) + lax.dot_general(
                normed[m, :, depth:], w_other[c], contract, preferred_element_type=jnp.float32
            )
            return carry

        lax.fori_loop(0, 4, one, 0)
        final[c] = part[c % 2, z]

    def up_copy(c, t):
        return remote(up_out.at[c, t], up_in.at[c, t], up_send.at[c, t], up_recv.at[c, t], gx, gy + 2)

    def down_copy(c, t):
        return remote(down_out.at[c, t], down_in.at[c, t], down_send.at[c, t], down_recv.at[c, t], gx, gy - 2)

    def forward_up(c, t):
        arrived(up_in.at[c, t], up_recv.at[c, t])
        up_out[c, t] = (part[c % 2, t] + up_in[c, t].astype(jnp.float32)).astype(jnp.bfloat16)
        up_copy(c, t).start()

    def forward_down(c, d):
        arrived(down_in.at[c, d], down_recv.at[c, d])
        down_out[c, d] = (part[c % 2, d] + down_in[c, d].astype(jnp.float32)).astype(jnp.bfloat16)
        down_copy(c, d).start()

    def second_hop(c):
        @pl.when(z == 2)
        def _():
            forward_up(c, 3)

        @pl.when(z == 1)
        def _():
            forward_down(c, 0)

    def pass_on(c, beside=None):
        for t in (3, 2, 1):
            d = 3 - t

            @pl.when(z == 0)
            def _():
                if t == 1:
                    up_copy(c, 3).wait_send()
                elif c > 0:
                    up_copy(c - 1, t - 1).wait_send()
                up_out[c, t] = part[c % 2, t].astype(jnp.bfloat16)
                up_copy(c, t).start()

            @pl.when(z == 3)
            def _():
                if t == 1:
                    down_copy(c, 0).wait_send()
                elif c > 0:
                    down_copy(c - 1, d + 1).wait_send()
                down_out[c, d] = part[c % 2, d].astype(jnp.bfloat16)
                down_copy(c, d).start()

            if t > 1:
                @pl.when(z == 1)
                def _():
                    forward_up(c, t)

                @pl.when(z == 2)
                def _():
                    forward_down(c, d)

            if t == 3 and c > 0:
                second_hop(c - 1)
            if beside is not None:
                beside(d)

    def finish(c):
        @pl.when(z > 0)
        def _():
            arrived(up_in.at[c, z], up_recv.at[c, z])
            final[c] = final[c] + up_in[c, z].astype(jnp.float32)

        @pl.when(z < 3)
        def _():
            arrived(down_in.at[c, z], down_recv.at[c, z])
            final[c] = final[c] + down_in[c, z].astype(jnp.float32)

    def rotated(u):
        return (u * cos_ref[...] + pltpu.roll(u, HD // 2, 1) * sin_ref[...]).astype(jnp.bfloat16)

    def q_chunk(c, beside):
        rows = pl.ds(pl.multiple_of((c - 1) * BLK, BLK), BLK)
        multiply(c, lambda: wq_ref[rows, :])
        pass_on(c, beside)

    def kv_up(step):
        block = kv_all.at[gy - 2 * step]
        return remote(block, block, kz_send.at[0, step], kv_recv.at[gy - 2 * step], gx, gy + 2)

    def kv_down(step):
        block = kv_all.at[gy + 2 * step]
        return remote(block, block, kz_send.at[1, step], kv_recv.at[gy + 2 * step], gx, gy - 2)

    def kv_across(source, side, step):
        return remote(kv_all.at[source], kv_all.at[source], ky_send.at[side, step], kv_recv.at[source], gx, y_peer)

    def kv_step(step, act):
        @pl.when((z >= step) & (z < 3))
        def _():
            act(kv_up(step))

        @pl.when((z + step <= 3) & (z > 0))
        def _():
            act(kv_down(step))

        if step == 0:
            act(kv_across(gy, 0, 0))
        else:
            @pl.when(z >= step)
            def _():
                act(kv_across(gy - 2 * step, 0, step))

            @pl.when(z + step <= 3)
            def _():
                act(kv_across(gy + 2 * step, 1, step))

    def kv_forward(step):
        @pl.when(z >= step)
        def _():
            arrived(kv_all.at[gy - 2 * step], kv_recv.at[gy - 2 * step])

        @pl.when(z + step <= 3)
        def _():
            arrived(kv_all.at[gy + 2 * step], kv_recv.at[gy + 2 * step])

        kv_step(step, lambda copy: copy.start())

    score_scale = math.log2(math.e) / math.sqrt(HD)
    keys = pl.ds(start_block, window)

    def attend(head):
        c = 1 + lax.div(head, 2)

        @pl.when(lax.rem(head, 2) == 0)
        def _():
            finish(c)

        lanes = pl.ds(pl.multiple_of(lax.rem(head, 2) * HD, HD), HD)
        query = rotated(final[c, :, lanes])
        key_rows = kv_all[keys, :, 0:HD].reshape(window * BLK, HD)
        value_rows = kv_all[keys, :, HD:].reshape(window * BLK, HD)
        scores = lax.dot_general(query, key_rows, contract, preferred_element_type=jnp.float32)
        scores = scores * score_scale + bias[...]
        weights = jnp.exp2(scores - jnp.max(scores, axis=1, keepdims=True))
        sums = jnp.sum(weights, axis=1, keepdims=True)
        mixed = jnp.dot(weights.astype(jnp.bfloat16), value_rows, preferred_element_type=jnp.float32)
        out_ref[:, pl.ds(pl.multiple_of(head * HD, HD), HD)] = (mixed / sums).astype(jnp.bfloat16)

    def share_kv(step):
        if step == 2:
            finish(0)
            kv_all[gy, :, 0:HD] = rotated(final[0, :, 0:HD])
            kv_all[gy, :, HD:] = final[0, :, HD:].astype(jnp.bfloat16)
            kv_step(0, lambda copy: copy.start())

    multiply(0, lambda: wkv_ref[kv_rows, :])
    pass_on(0)
    q_chunk(1, share_kv)
    q_chunk(2, lambda step: kv_forward(1) if step == 1 else None)
    q_chunk(3, lambda step: kv_forward(2 + step // 2) if step != 1 else None)

    def last_beside(step):
        if step == 0:
            for s in range(4):
                source = lax.rem(y_peer + 2 * s, 8)
                arrived(kv_all.at[source], kv_recv.at[source])
        attend(step)

    q_chunk(4, last_beside)
    second_hop(4)

    def late_head(head, carry):
        attend(head)
        return carry

    lax.fori_loop(3, 6, late_head, 0)

    page_len = cache_ref.shape[1]
    pages = slot_ref.shape[1]
    wanted = (gy * BLK + lax.broadcasted_iota(jnp.int32, (BLK, BLK), 0)).astype(jnp.float32)
    page = lax.broadcasted_iota(jnp.int32, (pages, BLK), 0)
    lane = lax.broadcasted_iota(jnp.int32, (pages, BLK), 1)
    offset = lax.rem(lane[0:8, :], page_len).astype(jnp.float32)
    slots = jnp.broadcast_to(slot_ref[...].astype(jnp.float32), (8, pages)).astype(jnp.bfloat16)
    picked = jnp.zeros((BLK, 2 * HD), jnp.float32)
    for s in range(8):
        spread = jnp.where(page == s * PAGES_DEV + lax.div(lane, page_len), 1.0, 0.0).astype(jnp.bfloat16)
        places = jnp.dot(slots, spread, preferred_element_type=jnp.float32) * page_len + offset
        chosen = jnp.where(places[0:1, :] == wanted, 1.0, 0.0).astype(jnp.bfloat16)
        picked = picked + jnp.dot(chosen, kv_all[s], preferred_element_type=jnp.float32)
    cache_ref[...] = picked.astype(jnp.bfloat16).reshape(cache_ref.shape)

    lax.fori_loop(6, 8, late_head, 0)

    for copy in sends:
        copy.wait_send()

    for step in range(4):
        kv_step(step, lambda copy: copy.wait_send())

    def drain(c, carry):
        for t in (3, 2):
            @pl.when((z > 0) & (z < t))
            def _():
                up_copy(c, t).wait_send()

            @pl.when((z < 3) & (z > 3 - t))
            def _():
                down_copy(c, 3 - t).wait_send()
        return carry

    lax.fori_loop(0, chunks, drain, 0)

    @pl.when(z == 0)
    def _():
        up_copy(chunks - 1, 2).wait_send()
        up_copy(chunks - 1, 1).wait_send()

    @pl.when(z == 3)
    def _():
        down_copy(chunks - 1, 1).wait_send()
        down_copy(chunks - 1, 2).wait_send()


def fused(hidden_in, norm_gain, query_proj, kv_proj, prompt_lengths, cache_slot):
    width = hidden_in.shape[1]
    query_cols = query_proj.shape[0]
    chunks = 1 + query_cols // BLK
    exponents = np.arange(HD // 2, dtype=np.float32) * 2.0 / HD
    frequency = np.float32(rope_base) ** -np.concatenate([exponents, exponents]).astype(np.float32)
    frequency = jnp.asarray(frequency[None, :])
    page_len = BLK // PAGES_DEV
    all_tokens = hidden_in.shape[0] * lax.axis_size("gx")
    window = all_tokens // 2 // BLK + 1
    bf16, f32 = jnp.bfloat16, jnp.float32
    dma = pltpu.SemaphoreType.DMA
    vmem = pl.BlockSpec(memory_space=pltpu.VMEM)
    return pl.pallas_call(
        fused_kernel,
        out_shape=(
            jax.ShapeDtypeStruct((BLK, query_cols), bf16),
            jax.ShapeDtypeStruct((PAGES_DEV, page_len, 2 * HD), bf16),
        ),
        in_specs=[vmem] * 7,
        out_specs=(vmem, vmem),
        scratch_shapes=[
            pltpu.VMEM((8, 8, 2 * BLK), f32),
            pltpu.VMEM((4, 8, 2 * BLK), f32),
            pltpu.VMEM((8, width), f32),
            pltpu.VMEM((8, width), f32),
            pltpu.VMEM((4, BLK, width), bf16),
            pltpu.VMEM((4, BLK, width), bf16),
            pltpu.VMEM((chunks, BLK, width), bf16),
            pltpu.VMEM((4, BLK, 2 * width), bf16),
            pltpu.VMEM((2, 4, BLK, BLK), f32),
            pltpu.VMEM((chunks, BLK, BLK), f32),
            pltpu.VMEM((chunks, 4, BLK, BLK), bf16),
            pltpu.VMEM((chunks, 4, BLK, BLK), bf16),
            pltpu.VMEM((chunks, 4, BLK, BLK), bf16),
            pltpu.VMEM((chunks, 4, BLK, BLK), bf16),
            pltpu.VMEM((8, BLK, 2 * HD), bf16),
            pltpu.VMEM((BLK, window * BLK), f32),
            pltpu.VMEM((BLK, HD), f32),
            pltpu.VMEM((BLK, HD), f32),
            dma((8,)), dma((8,)), dma((4,)), dma((4,)), dma((2,)), dma((7,)), dma((4,)), dma((4,)),
            dma((chunks,)), dma((chunks,)), dma((chunks, 4)), dma((chunks, 4)), dma((chunks, 4)), dma((chunks, 4)),
            dma((2, 4)), dma((2, 4)), dma((8,)),
        ],
        compiler_params=pltpu.CompilerParams(
            collective_id=0, has_side_effects=True, vmem_limit_bytes=56 * 1024 * 1024
        ),
        cost_estimate=pl.CostEstimate(flops=4000000000, bytes_accessed=8000000, transcendentals=3000000),
    )(
        prompt_lengths[None, :], cache_slot[None, :], hidden_in, norm_gain[None, :], frequency, query_proj, kv_proj
    )


def solution(mesh):
    form = fused if (mesh.shape["gx"], mesh.shape["gy"]) == (4, 8) else local
    return jax.shard_map(
        form,
        mesh=mesh,
        in_specs=(P("gx", "gy"), P("gy"), P("gx", "gy"), P(None, "gy"), P(), P()),
        out_specs=(P("gy", "gx"), P("gy", None, "gx")),
        check_vma=False,
    )
```
